512 devices in a mesh: gx: 16 (over y, core), gy: 32 (over z, x).
Axes of the slice: x: 4, y: 8, z: 8, core: 2. Of those that a mesh axis runs over, the one named last changes fastest.
Arguments:
- fine_nodes: bfloat16 [262144, 512], P(('gx', 'gy')), may hold values from -6 to 6
- fine_edges: bfloat16 [524288, 512], P(('gx', 'gy')), may hold values from -6 to 6
- edge_src: int32 [524288], P(('gx', 'gy')), may hold values from 0 to 767
- edge_dst: int32 [524288], P(('gx', 'gy')), may hold values from 0 to 511
- send_rows: int32 [512, 8, 32], P(('gx', 'gy')), may hold values from 0 to 512, as said below
- parents: int32 [262144], P(('gx', 'gy')), may hold values from 0 to 255
- coarse_src: int32 [32768], P('gy'), may hold values from 0 to 767
- coarse_dst: int32 [32768], P('gy'), may hold values from 0 to 255
- w_edge_in: bfloat16 [1536, 512], replicated, may hold values from -0.15625 to 0.15625
- w_edge_out: bfloat16 [512, 512], replicated, may hold values from -0.25 to 0.25
- edge_gain: float32 [512], replicated, may hold values from 0.1 to 1.9
- w_node_in: bfloat16 [1024, 512], replicated, may hold values from -0.1875 to 0.1875
- w_node_out: bfloat16 [512, 512], replicated, may hold values from -0.25 to 0.25
- node_gain: float32 [512], replicated, may hold values from 0.1 to 1.9
- w_cedge_in: bfloat16 [1024, 512], replicated, may hold values from -0.1875 to 0.1875
- w_cedge_out: bfloat16 [512, 512], replicated, may hold values from -0.25 to 0.25
- w_cnode_in: bfloat16 [1024, 512], replicated, may hold values from -0.1875 to 0.1875
- w_cnode_out: bfloat16 [512, 512], replicated, may hold values from -0.25 to 0.25
- coarse_gain: float32 [512], replicated, may hold values from 0.1 to 1.9
- w_up_in: bfloat16 [1024, 512], replicated, may hold values from -0.1875 to 0.1875
- w_up_out: bfloat16 [512, 512], replicated, may hold values from -0.25 to 0.25
- up_gain: float32 [512], replicated, may hold values from 0.1 to 1.9
Outputs:
- fine_out: bfloat16 [262144, 512], P(('gx', 'gy'))
- edges_out: bfloat16 [524288, 512], P(('gx', 'gy'))
The draws below stay inside these ranges and needn't reach their ends.
Inputs may be any that keep to these rules, and one draw needn't show every extreme that they name: `send_rows`: entries below 512 are local rows of the sending partition; 512 marks an empty slot; in each list the live entries come first, at least one is live, and some list is full.
All inputs are finite; a program needn't handle non-finite values.
Results may differ from the reference program's by a relative error of at most 0.015.
Values may be sent and summed in bfloat16 or wider, within the bound.
No kernel may reach another device: no remote copies, remote signals or barrier semaphores. Data moves between devices by JAX's collectives and lax.ppermute only.
A program may use at most 64 MiB of HBM per device.

```python
import jax
import jax.numpy as jnp
from jax import lax

D = 512
FINE = 512
CAP = 32
COARSE = 256
EDGE = 1024
CEDGE = 1024
GROUPS = 512
NODES = 262144
EDGES = 524288
CEDGES = 32768
N_GX = 16
N_GY = 32


def draw_send_rows(key, part):
    key = jax.random.fold_in(key, 11)
    key_count, key_rows = jax.random.split(key)
    counts = jax.random.randint(key_count, (GROUPS, 8, 1), 1, CAP + 1)
    counts = counts.at[0, 0, 0].set(CAP).at[0, 1, 0].set(1)
    rows = jax.random.randint(key_rows, (GROUPS, 8, CAP), 0, FINE)
    rows = rows.at[0, 0, 0].set(0)
    slot = jnp.arange(CAP, dtype=jnp.int32)[None, None, :]
    return jnp.where(slot < counts, rows, FINE).astype(jnp.int32)


def with_ends(drawn, stream_key, low, top_value):
    longest = drawn.shape.index(max(drawn.shape))
    spots = []
    for shift in (0, 1):
        where = [jax.random.randint(jax.random.fold_in(stream_key, axis), (), 0, length) for axis, length in enumerate(drawn.shape)]
        where[longest] = (where[longest] + shift) % drawn.shape[longest]
        spots.append(tuple(where))
    return drawn.at[spots[0]].set(low).at[spots[1]].set(top_value)


def steps_of(stream_key, dims, cuts, low, top_value):
    factor_of = 1.0
    for dim, shards_of in cuts:
        draws = jax.random.uniform(jax.random.fold_in(jax.random.fold_in(stream_key, 6), dim), (shards_of,), jnp.float32, low / len(cuts), top_value / len(cuts))
        factor_of = factor_of * jnp.repeat(jnp.exp(draws), dims[dim] // shards_of).reshape((-1,) + (1,) * (len(dims) - 1 - dim))
    return factor_of


def bell_draw(stream_key, dims, scale, most, cuts=(), held_as=jnp.bfloat16):
    result = scale * jax.random.normal(stream_key, dims, jnp.float32)
    if cuts:
        result = result * steps_of(stream_key, dims, cuts, -0.22, 0.18)
    return jnp.clip(result, -most, most).astype(held_as)


def setup_inputs(seed: int = 0) -> dict:
    splits = jax.random.split(jax.random.key(seed), 23)
    fine_nodes = bell_draw(splits[0], (NODES, D), 1.0, 6.0, ((0, 512),))
    fine_edges = bell_draw(splits[1], (EDGES, D), 1.0, 6.0, ((0, 512),))
    edge_src = with_ends(jax.random.randint(splits[2], (EDGES,), 0, FINE + 8 * CAP), jax.random.fold_in(splits[2], 1), 0, (FINE + 8 * CAP) - 1).astype(jnp.int32)
    edge_dst = with_ends(jax.random.randint(splits[3], (EDGES,), 0, FINE), jax.random.fold_in(splits[3], 1), 0, FINE - 1).astype(jnp.int32)
    send_rows = draw_send_rows(jax.random.fold_in(splits[22], 71), 0)
    parents = with_ends(jax.random.randint(splits[5], (NODES,), 0, COARSE), jax.random.fold_in(splits[5], 1), 0, COARSE - 1).astype(jnp.int32)
    coarse_src = with_ends(jax.random.randint(splits[6], (CEDGES,), 0, 3 * COARSE), jax.random.fold_in(splits[6], 1), 0, (3 * COARSE) - 1).astype(jnp.int32)
    coarse_dst = with_ends(jax.random.randint(splits[7], (CEDGES,), 0, COARSE), jax.random.fold_in(splits[7], 1), 0, COARSE - 1).astype(jnp.int32)
    w_edge_in = bell_draw(splits[8], (3 * D, D), (3 * D) ** -0.5, 0.15625)
    w_edge_out = bell_draw(splits[9], (D, D), D ** -0.5, 0.25)
    edge_gain = jnp.clip(1.0 + 0.18 * jax.random.normal(splits[10], (D,), jnp.float32), 0.1, 1.9)
    w_node_in = bell_draw(splits[11], (2 * D, D), (2 * D) ** -0.5, 0.1875)
    w_node_out = bell_draw(splits[12], (D, D), D ** -0.5, 0.25)
    node_gain = jnp.clip(1.0 + 0.18 * jax.random.normal(splits[13], (D,), jnp.float32), 0.1, 1.9)
    w_cedge_in = bell_draw(splits[14], (2 * D, D), (2 * D) ** -0.5, 0.1875)
    w_cedge_out = bell_draw(splits[15], (D, D), D ** -0.5, 0.25)
    w_cnode_in = bell_draw(splits[16], (2 * D, D), (2 * D) ** -0.5, 0.1875)
    w_cnode_out = bell_draw(splits[17], (D, D), D ** -0.5, 0.25)
    coarse_gain = jnp.clip(1.0 + 0.18 * jax.random.normal(splits[18], (D,), jnp.float32), 0.1, 1.9)
    w_up_in = bell_draw(splits[19], (2 * D, D), (2 * D) ** -0.5, 0.1875)
    w_up_out = bell_draw(splits[20], (D, D), D ** -0.5, 0.25)
    up_gain = jnp.clip(1.0 + 0.18 * jax.random.normal(splits[21], (D,), jnp.float32), 0.1, 1.9)
    return dict(fine_nodes=fine_nodes, fine_edges=fine_edges, edge_src=edge_src, edge_dst=edge_dst, send_rows=send_rows, parents=parents, coarse_src=coarse_src, coarse_dst=coarse_dst, w_edge_in=w_edge_in, w_edge_out=w_edge_out, edge_gain=edge_gain, w_node_in=w_node_in, w_node_out=w_node_out, node_gain=node_gain, w_cedge_in=w_cedge_in, w_cedge_out=w_cedge_out, w_cnode_in=w_cnode_in, w_cnode_out=w_cnode_out, coarse_gain=coarse_gain, w_up_in=w_up_in, w_up_out=w_up_out, up_gain=up_gain)


OFFSETS = ((-1, -1), (-1, 0), (-1, 1), (0, -1), (0, 1), (1, -1), (1, 0), (1, 1))

def layer_norm(values):
    mean = lax.optimization_barrier(jnp.mean(values, axis=-1, keepdims=True))
    centred = values - mean
    spread = lax.optimization_barrier(jnp.mean(centred * centred, axis=-1, keepdims=True))
    return centred * lax.rsqrt(spread + 1e-05)

def mlp_tail(pre, w_out, gain):
    act = jax.nn.silu(pre).astype(jnp.bfloat16)
    return layer_norm(jnp.dot(act, w_out, preferred_element_type=jnp.float32)) * gain

def reference(fine_nodes, fine_edges, edge_src, edge_dst, send_rows, parents, coarse_src, coarse_dst, w_edge_in, w_edge_out, edge_gain, w_node_in, w_node_out, node_gain, w_cedge_in, w_cedge_out, w_cnode_in, w_cnode_out, coarse_gain, w_up_in, w_up_out, up_gain):
    width = D
    ngx = N_GX
    ngy = N_GY
    groups = ngx * ngy
    src_proj = jnp.dot(fine_nodes, w_edge_in[width:2 * width], preferred_element_type=jnp.float32).astype(jnp.bfloat16)
    dst_proj = jnp.dot(fine_nodes, w_edge_in[2 * width:], preferred_element_type=jnp.float32).astype(jnp.bfloat16)
    src_proj = src_proj.reshape(groups, FINE, width)
    dst_proj = dst_proj.reshape(groups, FINE, width)
    padded = jnp.concatenate([src_proj, jnp.zeros((groups, 1, width), jnp.bfloat16)], 1)
    outgoing = jax.vmap(lambda rows_table, picks: rows_table[picks])(padded, send_rows)
    grid_out = outgoing.reshape(ngx, ngy, 8, CAP, width)
    arrivals = []
    for slot_list, (step_x, step_y) in enumerate(OFFSETS):
        framed = jnp.pad(grid_out[:, :, slot_list], ((1, 1), (1, 1), (0, 0), (0, 0)))
        arrivals.append(framed[1 - step_x:1 - step_x + ngx, 1 - step_y:1 - step_y + ngy])
    received = jnp.stack(arrivals, 2).reshape(groups, 8 * CAP, width)
    table = jnp.concatenate([src_proj, received], 1)
    nodes = fine_nodes.reshape(groups, FINE, width)
    edges = fine_edges.reshape(groups, EDGE, width)
    sources = edge_src.reshape(groups, EDGE)
    targets = edge_dst.reshape(groups, EDGE)

    def one_part(pieces):
        tab, dproj, node, edge, src_idx, dst_idx = pieces
        pre = jnp.dot(edge, w_edge_in[:width], preferred_element_type=jnp.float32)
        pre = pre + tab[src_idx].astype(jnp.float32) + dproj[dst_idx].astype(jnp.float32)
        message = mlp_tail(pre, w_edge_out, edge_gain)
        new_edge = (edge.astype(jnp.float32) + message).astype(jnp.bfloat16)
        summed = jax.ops.segment_sum(message, dst_idx, num_segments=FINE).astype(jnp.bfloat16)
        node_pre = jnp.dot(node, w_node_in[:width], preferred_element_type=jnp.float32)
        node_pre = node_pre + jnp.dot(summed, w_node_in[width:], preferred_element_type=jnp.float32)
        level = (node.astype(jnp.float32) + mlp_tail(node_pre, w_node_out, node_gain)).astype(jnp.bfloat16)
        return (level, new_edge)
    level_one, new_edges = lax.map(one_part, (table, dst_proj, nodes, edges, sources, targets))
    levels = level_one.reshape(ngx, ngy, FINE, width).transpose(1, 0, 2, 3)
    owner = parents.reshape(ngx, ngy, FINE)
    column_owner = owner.transpose(1, 0, 2)
    labels = jnp.arange(COARSE, dtype=jnp.int32)

    def pool_column(pieces):
        lev, own = pieces
        onehot = (own.reshape(-1)[:, None] == labels[None, :]).astype(jnp.bfloat16)
        return jnp.dot(onehot.T, lev.reshape(-1, width), preferred_element_type=jnp.float32)
    pooled = lax.map(pool_column, (levels, column_owner))
    coarse_zero = layer_norm(pooled).astype(jnp.bfloat16)
    flat_zero = coarse_zero.reshape(-1, width)
    side_src = jnp.dot(flat_zero, w_cedge_in[:width], preferred_element_type=jnp.float32).astype(jnp.bfloat16)
    side_dst = jnp.dot(flat_zero, w_cedge_in[width:], preferred_element_type=jnp.float32).astype(jnp.bfloat16)
    side_src = side_src.reshape(ngy, COARSE, width)
    side_dst = side_dst.reshape(ngy, COARSE, width)
    blank = jnp.zeros((1, COARSE, width), jnp.bfloat16)
    left = jnp.concatenate([blank, side_src[:-1]], 0)
    right = jnp.concatenate([side_src[1:], blank], 0)
    extended = jnp.concatenate([left, side_src, right], 1)
    csources = coarse_src.reshape(ngy, CEDGE)
    ctargets = coarse_dst.reshape(ngy, CEDGE)

    def coarse_part(pieces):
        ext, sdst, src_idx, dst_idx = pieces
        act = jax.nn.silu(ext[src_idx].astype(jnp.float32) + sdst[dst_idx].astype(jnp.float32)).astype(jnp.bfloat16)
        msg = layer_norm(jnp.dot(act, w_cedge_out, preferred_element_type=jnp.float32))
        return jax.ops.segment_sum(msg, dst_idx, num_segments=COARSE).astype(jnp.bfloat16)
    coarse_sum = lax.map(coarse_part, (extended, side_dst, csources, ctargets)).reshape(-1, width)
    cpre = jnp.dot(flat_zero, w_cnode_in[:width], preferred_element_type=jnp.float32)
    cpre = cpre + jnp.dot(coarse_sum, w_cnode_in[width:], preferred_element_type=jnp.float32)
    coarse_one = (flat_zero.astype(jnp.float32) + mlp_tail(cpre, w_cnode_out, coarse_gain)).astype(jnp.bfloat16)
    column = jnp.arange(ngy, dtype=jnp.int32)[None, :, None]
    lookup = (column * COARSE + owner).reshape(-1).astype(jnp.int32)
    lifted = coarse_one[lookup]
    flat_one = level_one.reshape(-1, width)
    upre = jnp.dot(flat_one, w_up_in[:width], preferred_element_type=jnp.float32)
    upre = upre + jnp.dot(lifted, w_up_in[width:], preferred_element_type=jnp.float32)
    fine_out = (flat_one.astype(jnp.float32) + mlp_tail(upre, w_up_out, up_gain)).astype(jnp.bfloat16)
    return (fine_out, new_edges.reshape(-1, width))
```

```python
import jax
import jax.numpy as jnp
from jax import lax
from jax.experimental import pallas as pl
from jax.experimental.pallas import tpu as pltpu
from jax.sharding import PartitionSpec as P

COARSE = 256
OFFSETS = ((-1, -1), (-1, 0), (-1, 1), (0, -1), (0, 1), (1, -1), (1, 0), (1, 1))
BF16 = jnp.bfloat16
F32 = jnp.float32


def dot(a, b):
    return jnp.dot(a, b, preferred_element_type=F32)


def silu(v):
    return v / (1.0 + jnp.exp(-v))


def layer_norm(values):
    mean = jnp.mean(values, axis=-1, keepdims=True)
    centred = values - mean
    spread = jnp.mean(centred * centred, axis=-1, keepdims=True)
    return centred * lax.rsqrt(spread + 1e-05)


def mlp_tail(pre, w_out, gain):
    return layer_norm(dot(silu(pre).astype(BF16), w_out)) * gain


def pick(column, width, base=0):
    lanes = lax.broadcasted_iota(jnp.int32, (column.shape[0], width), 1) + base
    return jnp.where(lanes == column, 1.0, 0.0).astype(BF16)


def spread(row, height):
    rows = lax.broadcasted_iota(jnp.int32, (height, row.shape[1]), 0)
    return jnp.where(rows == row, 1.0, 0.0).astype(BF16)


def columns(table, start, count):
    return jnp.concatenate([table[:, k : k + 1] for k in range(start, start + count)], 0)


def outgoing_kernel(nodes, lists, out):
    picks = jnp.transpose(lists[...])
    nodes = nodes[...]
    for k in range(8):
        out[32 * k : 32 * k + 32, :] = dot(pick(picks[:, k : k + 1], 512), nodes).astype(BF16)


def before_halo_kernel(nodes, edges, src, dst, w_in, w_node, pre, node_pre):
    nodes = nodes[...]
    src_proj = dot(nodes, w_in[512:1024, :]).astype(BF16)
    dst_proj = dot(nodes, w_in[1024:1536, :]).astype(BF16)
    src_t, dst_t = jnp.transpose(src[...]), jnp.transpose(dst[...])
    for c in range(4):
        rows = slice(256 * c, 256 * c + 256)
        part = dot(edges[rows, :], w_in[0:512, :])
        part = part + dot(pick(columns(src_t, 2 * c, 2), 512), src_proj)
        pre[rows, :] = part + dot(pick(columns(dst_t, 2 * c, 2), 512), dst_proj)
    node_pre[...] = dot(nodes, w_node[0:512, :])


def after_halo_kernel(
    received, pre, node_pre, nodes, edges, src, dst, parents,
    w_in, w_out, gain, w_node, w_node_out, node_gain,
    edges_out, level_one, pooled, total,
):
    halo = dot(received[...], w_in[512:1024, :]).astype(BF16)
    src_t = jnp.transpose(src[...])
    for c in range(4):
        rows = slice(256 * c, 256 * c + 256)
        part = pre[rows, :] + dot(pick(columns(src_t, 2 * c, 2), 256, 512), halo)
        message = mlp_tail(part, w_out[...], gain[...])
        edges_out[rows, :] = (edges[rows, :].astype(F32) + message).astype(BF16)
        target = jnp.concatenate([dst[2 * c : 2 * c + 1, :], dst[2 * c + 1 : 2 * c + 2, :]], 1)
        added = dot(spread(target, 512), message.astype(BF16))
        if c == 0:
            total[...] = added
        else:
            total[...] += added
    summed = total[...].astype(BF16)
    part = node_pre[...] + dot(summed, w_node[512:1024, :])
    level = nodes[...].astype(F32) + mlp_tail(part, w_node_out[...], node_gain[...])
    level = level.astype(BF16)
    level_one[...] = level
    owner = jnp.concatenate([parents[k : k + 1, :] for k in range(4)], 1)
    pooled[...] = dot(spread(owner, COARSE), level).astype(BF16)


def share_kernel(parts, out):
    total = parts[0].astype(F32)
    for k in range(1, parts.shape[0]):
        total = total + parts[k].astype(F32)
    out[...] = layer_norm(total).astype(BF16)


def up_first_kernel(level_one, w_up, out):
    out[...] = dot(level_one[...], w_up[0:512, :])


def coarse_kernel(
    zero, csrc, cdst, parents, level_one, up_pre,
    w_cin, w_cout, w_nin, w_nout, coarse_gain, w_up, w_up_out, up_gain,
    out, total,
):
    side_src = dot(zero[...], w_cin[0:512, :]).astype(BF16)
    own = zero[256:512, :]
    side_dst = dot(own, w_cin[512:1024, :]).astype(BF16)
    src_t, dst_t = jnp.transpose(csrc[...]), jnp.transpose(cdst[...])
    for c in range(4):
        part = dot(pick(columns(src_t, 2 * c, 2), 768), side_src)
        part = part + dot(pick(columns(dst_t, 2 * c, 2), 256), side_dst)
        message = layer_norm(dot(silu(part).astype(BF16), w_cout[...]))
        target = jnp.concatenate([cdst[2 * c : 2 * c + 1, :], cdst[2 * c + 1 : 2 * c + 2, :]], 1)
        added = dot(spread(target, COARSE), message.astype(BF16))
        if c == 0:
            total[...] = added
        else:
            total[...] += added
    summed = total[...].astype(BF16)
    part = dot(own, w_nin[0:512, :]) + dot(summed, w_nin[512:1024, :])
    one = (own.astype(F32) + mlp_tail(part, w_nout[...], coarse_gain[...])).astype(BF16)
    owner_t = jnp.transpose(parents[...])
    for c in range(2):
        rows = slice(256 * c, 256 * c + 256)
        lifted = dot(pick(columns(owner_t, 2 * c, 2), COARSE), one).astype(BF16)
        part = up_pre[rows, :] + dot(lifted, w_up[512:1024, :])
        tail = mlp_tail(part, w_up_out[...], up_gain[...])
        out[rows, :] = (level_one[rows, :].astype(F32) + tail).astype(BF16)


def call(kernel, outs, *args, scratch=(), flops=0, name=None):
    shapes = [jax.ShapeDtypeStruct(s, d) for s, d in outs]
    moved = sum(a.size * a.dtype.itemsize for a in args) + sum(s.size * s.dtype.itemsize for s in shapes)
    result = pl.pallas_call(
        kernel,
        out_shape=shapes,
        in_specs=[pl.BlockSpec(memory_space=pltpu.VMEM)] * len(args),
        out_specs=[pl.BlockSpec(memory_space=pltpu.VMEM)] * len(shapes),
        scratch_shapes=list(scratch),
        compiler_params=pltpu.CompilerParams(vmem_limit_bytes=48 * 1024 * 1024),
        cost_estimate=pl.CostEstimate(flops=flops, bytes_accessed=moved, transcendentals=0),
        name=name,
    )(*args)
    return result if len(result) > 1 else result[0]


def grid_pairs(step_x, step_y, count_x, count_y):
    pairs = []
    for i in range(count_x):
        for j in range(count_y):
            a, b = i + step_x, j + step_y
            if 0 <= a < count_x and 0 <= b < count_y:
                pairs.append((i * count_y + j, a * count_y + b))
    return pairs


def per_device(
    fine_nodes, fine_edges, edge_src, edge_dst, send_rows, parents, coarse_src, coarse_dst,
    w_edge_in, w_edge_out, edge_gain, w_node_in, w_node_out, node_gain, w_cedge_in, w_cedge_out,
    w_cnode_in, w_cnode_out, coarse_gain, w_up_in, w_up_out, up_gain,
):
    count_x, count_y = lax.axis_size("gx"), lax.axis_size("gy")
    src, dst = edge_src.reshape(8, 128), edge_dst.reshape(8, 128)
    csrc, cdst = coarse_src.reshape(8, 128), coarse_dst.reshape(8, 128)
    owner = parents.reshape(4, 128)
    edge_gain, node_gain = edge_gain.reshape(1, 512), node_gain.reshape(1, 512)
    coarse_gain, up_gain = coarse_gain.reshape(1, 512), up_gain.reshape(1, 512)

    outgoing = call(
        outgoing_kernel, [((256, 512), BF16)], fine_nodes, send_rows[0],
        flops=2 * 256 * 512 * 512, name="outgoing",
    )
    received = [
        lax.ppermute(
            outgoing[32 * k : 32 * k + 32], ("gx", "gy"), grid_pairs(dx, dy, count_x, count_y)
        )
        for k, (dx, dy) in enumerate(OFFSETS)
    ]
    received = jnp.concatenate(received, 0)
    pre, node_pre = call(
        before_halo_kernel, [((1024, 512), F32), ((512, 512), F32)],
        fine_nodes, fine_edges, src, dst, w_edge_in, w_node_in,
        flops=2 * 9 * 512**3, name="before_halo",
    )
    edges_out, level_one, pooled = call(
        after_halo_kernel, [((1024, 512), BF16), ((512, 512), BF16), ((COARSE, 512), BF16)],
        received, pre, node_pre, fine_nodes, fine_edges, src, dst, owner,
        w_edge_in, w_edge_out, edge_gain, w_node_in, w_node_out, node_gain,
        scratch=[pltpu.VMEM((512, 512), F32)], flops=2 * 8 * 512**3, name="after_halo",
    )
    parts = lax.all_to_all(pooled, "gx", 0, 0, tiled=True)
    share = call(
        share_kernel, [((COARSE // count_x, 512), BF16)], parts.reshape(count_x, -1, 512),
        flops=COARSE * 512, name="share",
    )
    up = [(j, j + 1) for j in range(count_y - 1)]
    down = [(j + 1, j) for j in range(count_y - 1)]
    left = lax.ppermute(share, "gy", up)
    right = lax.ppermute(share, "gy", down)
    trio = jnp.stack([left, share, right])
    zero = lax.all_gather(trio, "gx", axis=1, tiled=True).reshape(768, 512)
    up_pre = call(up_first_kernel, [((512, 512), F32)], level_one, w_up_in, flops=2 * 512**3, name="up_first")
    fine_out = call(
        coarse_kernel, [((512, 512), BF16)],
        zero, csrc, cdst, owner, level_one, up_pre,
        w_cedge_in, w_cedge_out, w_cnode_in, w_cnode_out, coarse_gain, w_up_in, w_up_out, up_gain,
        scratch=[pltpu.VMEM((COARSE, 512), F32)], flops=2 * 14 * 512**3, name="coarse",
    )
    return fine_out, edges_out


def solution(mesh):
    fine, flat = P(("gx", "gy"), None), P(("gx", "gy"))
    return jax.shard_map(
        per_device,
        mesh=mesh,
        in_specs=(fine, fine, flat, flat, P(("gx", "gy"), None, None), flat, P("gy"), P("gy")) + (P(),) * 14,
        out_specs=(fine, fine),
        check_vma=False,
    )
```

```python
import jax
import jax.numpy as jnp
from jax import lax
from jax.experimental import pallas as pl
from jax.experimental.pallas import tpu as pltpu
from jax.sharding import PartitionSpec as P

COARSE = 256
CHUNK = 1024
BF16 = jnp.bfloat16
F32 = jnp.float32


def dot(a, b):
    return jnp.dot(a, b, preferred_element_type=F32)


def silu(v):
    half = 0.5 * v
    return half + half * jnp.tanh(half)


def layer_norm(values):
    mean = jnp.mean(values, axis=-1, keepdims=True)
    centred = values - mean
    spread = jnp.mean(centred * centred, axis=-1, keepdims=True)
    return centred * lax.rsqrt(spread + 1e-05)


def mlp_tail(pre, w_out, gain):
    return layer_norm(dot(silu(pre).astype(BF16), w_out)) * gain


def pick(column, width, base=0):
    lanes = lax.broadcasted_iota(jnp.int32, (column.shape[0], width), 1) + base
    return jnp.where(lanes == column, 1.0, 0.0).astype(BF16)


def spread(row, height):
    rows = lax.broadcasted_iota(jnp.int32, (height, row.shape[1]), 0)
    return jnp.where(rows == row, 1.0, 0.0).astype(BF16)


def columns(table, start, count):
    return jnp.concatenate([table[:, k : k + 1] for k in range(start, start + count)], 0)


def outgoing_kernel(nodes, lists, before, left, right, after):
    picks = jnp.transpose(lists[...])
    nodes = nodes[...]
    picked = dot(jnp.concatenate([pick(picks[:, k : k + 1], 512) for k in range(8)], 0), nodes)
    picked = picked.astype(BF16)
    before[...] = picked[0:96, :]
    left[...] = picked[96:128, :]
    right[...] = picked[128:160, :]
    after[...] = picked[160:256, :]


def tables_kernel(nodes, src, dst, w_in, gathered):
    nodes = nodes[...]
    src_proj = dot(nodes, w_in[512:1024, :]).astype(BF16)
    dst_proj = dot(nodes, w_in[1024:1536, :]).astype(BF16)
    src_t, dst_t = jnp.transpose(src[...]), jnp.transpose(dst[...])
    for c in range(1024 // CHUNK):
        rows = slice(CHUNK * c, CHUNK * c + CHUNK)
        part = dot(pick(columns(src_t, CHUNK // 128 * c, CHUNK // 128), 512), src_proj)
        gathered[rows, :] = part + dot(pick(columns(dst_t, CHUNK // 128 * c, CHUNK // 128), 512), dst_proj)


def edges_kernel(nodes, edges, gathered, w_in, w_node, pre, node_pre):
    pre[...] = gathered[...] + dot(edges[...], w_in[0:512, :])
    node_pre[...] = dot(nodes[...], w_node[0:512, :])


def after_halo_kernel(
    above, below, from_right, from_left, pre, node_pre, nodes, edges, src, dst, parents,
    w_in, w_out, gain, w_node, w_node_out, node_gain,
    edges_out, level_one, pooled, total,
):
    received = jnp.concatenate(
        [
            from_right[0:32, :], above[32:64, :], from_left[0:32, :], from_right[32:64, :],
            from_left[32:64, :], from_right[64:96, :], below[32:64, :], from_left[64:96, :],
        ],
        0,
    )
    halo = dot(received, w_in[512:1024, :]).astype(BF16)
    src_t = jnp.transpose(src[...])
    for c in range(1024 // CHUNK):
        rows = slice(CHUNK * c, CHUNK * c + CHUNK)
        part = pre[rows, :] + dot(pick(columns(src_t, CHUNK // 128 * c, CHUNK // 128), 256, 512), halo)
        message = mlp_tail(part, w_out[...], gain[...])
        edges_out[rows, :] = (edges[rows, :].astype(F32) + message).astype(BF16)
        target = jnp.concatenate([dst[k : k + 1, :] for k in range(CHUNK // 128 * c, CHUNK // 128 * (c + 1))], 1)
        added = dot(spread(target, 512), message.astype(BF16))
        if c == 0:
            total[...] = added
        else:
            total[...] += added
    summed = total[...].astype(BF16)
    part = node_pre[...] + dot(summed, w_node[512:1024, :])
    level = nodes[...].astype(F32) + mlp_tail(part, w_node_out[...], node_gain[...])
    level = level.astype(BF16)
    level_one[...] = level
    owner = jnp.concatenate([parents[k : k + 1, :] for k in range(4)], 1)
    pooled[...] = dot(spread(owner, COARSE), level).astype(BF16)


def share_kernel(parts, out):
    total = parts[0].astype(F32)
    for k in range(1, parts.shape[0]):
        total = total + parts[k].astype(F32)
    share = layer_norm(total).astype(BF16)
    for k in range(out.shape[0]):
        out[k] = share


def own_kernel(
    zero, csrc, cdst, level_one, w_cin, w_nin, w_up, pre, node_pre, up_pre
):
    zero = zero[...]
    side_src = dot(zero, w_cin[0:512, :]).astype(BF16)
    side_dst = dot(zero, w_cin[512:1024, :]).astype(BF16)
    src_t, dst_t = jnp.transpose(csrc[...]), jnp.transpose(cdst[...])
    for c in range(1024 // CHUNK):
        rows = slice(CHUNK * c, CHUNK * c + CHUNK)
        part = dot(pick(columns(src_t, CHUNK // 128 * c, CHUNK // 128), COARSE, COARSE), side_src)
        pre[rows, :] = part + dot(pick(columns(dst_t, CHUNK // 128 * c, CHUNK // 128), COARSE), side_dst)
    node_pre[...] = dot(zero, w_nin[0:512, :])
    up_pre[...] = dot(level_one[...], w_up[0:512, :])


def coarse_kernel(
    left, right, zero, pre, node_pre, up_pre, csrc, cdst, parents, level_one,
    w_cin, w_cout, w_nin, w_nout, coarse_gain, w_up, w_up_out, up_gain,
    out, total,
):
    sides = dot(jnp.concatenate([left[...], right[...]], 0), w_cin[0:512, :]).astype(BF16)
    src = csrc[...]
    src_t = jnp.transpose(jnp.where(src < 256, src, src - 256))
    src_t = jnp.where(jnp.transpose((src >> 8)) == 1, -1, src_t)
    for c in range(1024 // CHUNK):
        rows = slice(CHUNK * c, CHUNK * c + CHUNK)
        part = pre[rows, :] + dot(pick(columns(src_t, CHUNK // 128 * c, CHUNK // 128), 512), sides)
        message = layer_norm(dot(silu(part).astype(BF16), w_cout[...]))
        target = jnp.concatenate([cdst[k : k + 1, :] for k in range(CHUNK // 128 * c, CHUNK // 128 * (c + 1))], 1)
        added = dot(spread(target, COARSE), message.astype(BF16))
        if c == 0:
            total[...] = added
        else:
            total[...] += added
    summed = total[...].astype(BF16)
    part = node_pre[...] + dot(summed, w_nin[512:1024, :])
    one = (zero[...].astype(F32) + mlp_tail(part, w_nout[...], coarse_gain[...])).astype(BF16)
    owner_t = jnp.transpose(parents[...])
    for c in range(2):
        rows = slice(256 * c, 256 * c + 256)
        lifted = dot(pick(columns(owner_t, 2 * c, 2), COARSE), one).astype(BF16)
        part = up_pre[rows, :] + dot(lifted, w_up[512:1024, :])
        tail = mlp_tail(part, w_up_out[...], up_gain[...])
        out[rows, :] = (level_one[rows, :].astype(F32) + tail).astype(BF16)


def kept(shape, dtype):
    return pltpu.VMEM(shape, dtype)


def call(kernel, outs, *args, scratch=(), flops=0, name=None):
    shapes = [kept(s, d) if d == F32 else jax.ShapeDtypeStruct(s, d) for s, d in outs]
    args = [pltpu.with_memory_space_constraint(a, pltpu.VMEM) if a.dtype == F32 and a.shape[0] > 1 else a for a in args]
    moved = sum(a.size * a.dtype.itemsize for a in args)
    result = pl.pallas_call(
        kernel,
        out_shape=shapes,
        in_specs=[pl.BlockSpec(memory_space=pltpu.VMEM)] * len(args),
        out_specs=[pl.BlockSpec(memory_space=pltpu.VMEM)] * len(shapes),
        scratch_shapes=list(scratch),
        compiler_params=pltpu.CompilerParams(vmem_limit_bytes=48 * 1024 * 1024),
        cost_estimate=pl.CostEstimate(flops=flops, bytes_accessed=moved, transcendentals=0),
        name=name,
    )(*args)
    return result if len(result) > 1 else result[0]


def steps(count):
    up = [(k, k + 1) for k in range(count - 1)]
    return up, [(b, a) for a, b in up]


def per_device(
    fine_nodes, fine_edges, edge_src, edge_dst, send_rows, parents, coarse_src, coarse_dst,
    w_edge_in, w_edge_out, edge_gain, w_node_in, w_node_out, node_gain, w_cedge_in, w_cedge_out,
    w_cnode_in, w_cnode_out, coarse_gain, w_up_in, w_up_out, up_gain,
):
    count_x, count_y = lax.axis_size("gx"), lax.axis_size("gy")
    src, dst = edge_src.reshape(8, 128), edge_dst.reshape(8, 128)
    csrc, cdst = coarse_src.reshape(8, 128), coarse_dst.reshape(8, 128)
    owner = parents.reshape(4, 128)
    edge_gain, node_gain = edge_gain.reshape(1, 512), node_gain.reshape(1, 512)
    coarse_gain, up_gain = coarse_gain.reshape(1, 512), up_gain.reshape(1, 512)

    before, left, right, after = call(
        outgoing_kernel, [((96, 512), BF16), ((32, 512), BF16), ((32, 512), BF16), ((96, 512), BF16)],
        fine_nodes, send_rows[0], flops=100 * 2 * 256 * 512 * 512, name="outgoing",
    )
    up_x, down_x = steps(count_x)
    up_y, down_y = steps(count_y)
    above = lax.ppermute(before, "gx", down_x)
    below = lax.ppermute(after, "gx", up_x)
    gathered = call(
        tables_kernel, [((1024, 512), F32)], fine_nodes, src, dst, w_edge_in, flops=2 * 6 * 512**3, name="tables"
    )
    above, below, gathered = lax.optimization_barrier((above, below, gathered))
    from_right = lax.ppermute(jnp.concatenate([above[0:32], left, below[0:32]], 0), "gy", down_y)
    from_left = lax.ppermute(jnp.concatenate([above[64:96], right, below[64:96]], 0), "gy", up_y)
    pre, node_pre = call(
        edges_kernel, [((1024, 512), F32), ((512, 512), F32)],
        fine_nodes, fine_edges, gathered, w_edge_in, w_node_in, flops=2 * 3 * 512**3, name="edges",
    )
    edges_out, level_one, pooled = call(
        after_halo_kernel, [((1024, 512), BF16), ((512, 512), BF16), ((COARSE, 512), BF16)],
        above, below, from_right, from_left, pre, node_pre, fine_nodes, fine_edges, src, dst, owner,
        w_edge_in, w_edge_out, edge_gain, w_node_in, w_node_out, node_gain,
        scratch=[pltpu.VMEM((512, 512), F32)], flops=2 * 8 * 512**3, name="after_halo",
    )
    parts = lax.all_to_all(pooled, "gx", 0, 0, tiled=True)
    shares = call(
        share_kernel, [((count_x, COARSE // count_x, 512), BF16)], parts.reshape(count_x, -1, 512),
        flops=COARSE * 512, name="share",
    )
    zero = lax.all_to_all(shares, "gx", 0, 0, tiled=True).reshape(COARSE, 512)
    left, right = lax.ppermute(zero, "gy", up_y), lax.ppermute(zero, "gy", down_y)
    pre, node_pre, up_pre = call(
        own_kernel, [((1024, 512), F32), ((COARSE, 512), F32), ((512, 512), F32)],
        zero, csrc, cdst, level_one, w_cedge_in, w_cnode_in, w_up_in,
        flops=2 * 5 * 512**3, name="own_column",
    )
    fine_out = call(
        coarse_kernel, [((512, 512), BF16)],
        left, right, zero, pre, node_pre, up_pre, csrc, cdst, owner, level_one,
        w_cedge_in, w_cedge_out, w_cnode_in, w_cnode_out, coarse_gain, w_up_in, w_up_out, up_gain,
        scratch=[pltpu.VMEM((COARSE, 512), F32)], flops=2 * 9 * 512**3, name="coarse",
    )
    return fine_out, edges_out


def solution(mesh):
    fine, flat = P(("gx", "gy"), None), P(("gx", "gy"))
    return jax.shard_map(
        per_device,
        mesh=mesh,
        in_specs=(fine, fine, flat, flat, P(("gx", "gy"), None, None), flat, P("gy"), P("gy")) + (P(),) * 14,
        out_specs=(fine, fine),
        check_vma=False,
    )
```

```python
import jax
import jax.numpy as jnp
from jax import lax
from jax.experimental import pallas as pl
from jax.experimental.pallas import tpu as pltpu
from jax.sharding import PartitionSpec as P

COARSE = 256
BF16 = jnp.bfloat16
F32 = jnp.float32
I32 = jnp.int32


def dot(a, b):
    return jnp.dot(a, b, preferred_element_type=F32)


def silu(v):
    half = 0.5 * v
    return half + half * jnp.tanh(half)


def layer_norm(values):
    mean = jnp.mean(values, axis=-1, keepdims=True)
    centred = values - mean
    spread = jnp.mean(centred * centred, axis=-1, keepdims=True)
    return centred * lax.rsqrt(spread + 1e-05)


def mlp_tail(pre, w_out, gain):
    return layer_norm(dot(silu(pre).astype(BF16), w_out)) * gain


def pick(column, width, base=0):
    lanes = lax.broadcasted_iota(I32, (column.shape[0], width), 1) + base
    return jnp.where(lanes == column, 1.0, 0.0).astype(BF16)


def spread(row, height):
    rows = lax.broadcasted_iota(I32, (height, row.shape[1]), 0)
    return jnp.where(rows == row, 1.0, 0.0).astype(BF16)


def as_column(table):
    turned = jnp.transpose(table)
    return jnp.concatenate([turned[:, k : k + 1] for k in range(table.shape[0])], 0)


def as_row(table):
    return jnp.concatenate([table[k : k + 1, :] for k in range(table.shape[0])], 1)


def odd_place():
    return lax.axis_index("gx") % 2 == 1, lax.axis_index("gy") % 2 == 1


def fetch(sems, *pairs):
    copies = [pltpu.make_async_copy(a, b, sems.at[k]) for k, (a, b) in enumerate(pairs)]
    for copy in copies:
        copy.start()
    return copies


def outgoing_kernel(nodes_hbm, lists_hbm, far, before, after, near, nodes, lists, sems):
    got_lists, got_nodes = fetch(sems, (lists_hbm, lists), (nodes_hbm, nodes))
    got_lists.wait()
    odd_x, odd_y = odd_place()
    rows = lists[...]
    rows = jnp.where(odd_x, jnp.concatenate([rows[5:8], rows[3:5], rows[0:3]], 0), rows)
    rows = jnp.where(odd_y, jnp.concatenate([rows[k : k + 1] for k in (2, 1, 0, 4, 3, 7, 6, 5)], 0), rows)
    picks = jnp.transpose(rows)
    picks = jnp.concatenate([pick(picks[:, k : k + 1], 512) for k in range(8)], 0)
    got_nodes.wait()
    picked = dot(picks, nodes[...]).astype(BF16)
    far[...] = picked[0:96, :]
    before[...] = picked[96:128, :]
    after[...] = picked[128:160, :]
    near[...] = picked[160:256, :]


def tables_kernel(nodes, src, dst, w_in, gathered):
    nodes = nodes[...]
    src_proj = dot(nodes, w_in[512:1024, :]).astype(BF16)
    dst_proj = dot(nodes, w_in[1024:1536, :]).astype(BF16)
    part = dot(pick(as_column(src[...]), 512), src_proj)
    gathered[...] = part + dot(pick(as_column(dst[...]), 512), dst_proj)


def edges_kernel(
    nodes, gathered, edges_hbm, w_in_hbm, w_node_hbm, pre, node_pre, edges, w_source, w_summed, w_in, w_node, sems
):
    got = fetch(
        sems, (w_node_hbm.at[0:512], w_node), (w_in_hbm.at[0:512], w_in),
        (edges_hbm.at[0:512], edges.at[0:512]), (edges_hbm.at[512:1024], edges.at[512:1024]),
        (w_in_hbm.at[512:1024], w_source), (w_node_hbm.at[512:1024], w_summed),
    )
    got[0].wait()
    node_pre[...] = dot(nodes[...], w_node[...])
    got[1].wait()
    for c in range(2):
        rows = slice(512 * c, 512 * c + 512)
        got[2 + c].wait()
        pre[rows, :] = gathered[rows, :] + dot(edges[rows, :], w_in[...])
    got[4].wait()
    got[5].wait()


def after_halo_kernel(
    far, near, side_a, side_b, pre, node_pre, nodes, edges, src, dst, parents,
    w_source, w_out, gain, w_summed, w_node_out, node_gain,
    edges_hbm, level_one, pooled, edges_out, sems,
):
    received = jnp.concatenate(
        [
            side_a[64:96, :], near[32:64, :], side_b[64:96, :], side_a[32:64, :],
            side_b[32:64, :], side_a[0:32, :], far[32:64, :], side_b[0:32, :],
        ],
        0,
    )
    halo = dot(received, w_source[...]).astype(BF16)
    odd_x, odd_y = odd_place()
    slot = src[...] - 512
    k = slot >> 5
    turn_x = jnp.where(k < 3, k + 5, jnp.where(k > 4, k - 5, k))
    k = jnp.where(odd_x, turn_x, k)
    turn_y = jnp.where(
        (k == 0) | (k == 5), k + 2, jnp.where((k == 2) | (k == 7), k - 2, jnp.where(k == 3, 4, jnp.where(k == 4, 3, k)))
    )
    k = jnp.where(odd_y, turn_y, k)
    slot = jnp.where(slot < 0, -1, k * 32 + (slot & 31))
    part = pre[...] + dot(pick(as_column(slot), 256), halo)
    message = mlp_tail(part, w_out[...], gain[...])
    edges_out[...] = (edges[...].astype(F32) + message).astype(BF16)
    (sent,) = fetch(sems, (edges_out, edges_hbm))
    summed = dot(spread(as_row(dst[...]), 512), message.astype(BF16)).astype(BF16)
    part = node_pre[...] + dot(summed, w_summed[...])
    level = nodes[...].astype(F32) + mlp_tail(part, w_node_out[...], node_gain[...])
    level = level.astype(BF16)
    level_one[...] = level
    pooled[...] = dot(spread(as_row(parents[...]), COARSE), level).astype(BF16)
    sent.wait()


def share_kernel(parts, out):
    total = parts[0].astype(F32)
    for k in range(1, parts.shape[0]):
        total = total + parts[k].astype(F32)
    share = layer_norm(total).astype(BF16)
    for k in range(out.shape[0]):
        out[k] = share


def own_kernel(
    zero, csrc, cdst, level_one, w_cin, w_cin_hbm, w_nin_hbm, w_up_hbm, w_up_out_hbm,
    pre, node_pre, up_pre, w_source, w_summed, w_lifted, w_up_out, w_nin, w_up, sems,
):
    got = fetch(
        sems, (w_nin_hbm.at[0:512], w_nin), (w_up_hbm.at[0:512], w_up), (w_cin_hbm.at[0:512], w_source),
        (w_nin_hbm.at[512:1024], w_summed), (w_up_hbm.at[512:1024], w_lifted), (w_up_out_hbm, w_up_out),
    )
    zero = zero[...]
    side_src = dot(zero, w_cin[0:512, :]).astype(BF16)
    side_dst = dot(zero, w_cin[512:1024, :]).astype(BF16)
    part = dot(pick(as_column(csrc[...]), COARSE, COARSE), side_src)
    pre[...] = part + dot(pick(as_column(cdst[...]), COARSE), side_dst)
    got[0].wait()
    node_pre[...] = dot(zero, w_nin[...])
    got[1].wait()
    up_pre[...] = dot(level_one[...], w_up[...])
    for copy in got[2:]:
        copy.wait()


def coarse_kernel(
    left, right, zero, pre, node_pre, up_pre, csrc, cdst, parents, level_one,
    w_source, w_cout, w_summed, w_nout, coarse_gain, w_lifted, w_up_out, up_gain,
    out_hbm, out, sems,
):
    sides = dot(jnp.concatenate([left[...], right[...]], 0), w_source[...]).astype(BF16)
    src = csrc[...]
    src = jnp.where(src < COARSE, src, jnp.where(src < 2 * COARSE, -1, src - COARSE))
    part = pre[...] + dot(pick(as_column(src), 2 * COARSE), sides)
    message = layer_norm(dot(silu(part).astype(BF16), w_cout[...]))
    summed = dot(spread(as_row(cdst[...]), COARSE), message.astype(BF16)).astype(BF16)
    part = node_pre[...] + dot(summed, w_summed[...])
    one = (zero[...].astype(F32) + mlp_tail(part, w_nout[...], coarse_gain[...])).astype(BF16)
    lifted = dot(pick(as_column(parents[...]), COARSE), one).astype(BF16)
    part = up_pre[...] + dot(lifted, w_lifted[...])
    tail = mlp_tail(part, w_up_out[...], up_gain[...])
    out[...] = (level_one[...].astype(F32) + tail).astype(BF16)
    (sent,) = fetch(sems, (out, out_hbm))
    sent.wait()


def kept(shape, dtype):
    return pltpu.VMEM(shape, dtype)


def hold(array):
    return pltpu.with_memory_space_constraint(array, pltpu.VMEM)


def call(kernel, outs, *args, hbm=(), hbm_outs=(), held=(), scratch=(), copies=0, flops=0, name=None):
    shapes = [kept(s, d) if k in held else jax.ShapeDtypeStruct(s, d) for k, (s, d) in enumerate(outs)]
    args = list(args)
    hbm = [pltpu.with_memory_space_constraint(a, pltpu.HBM) for a in hbm]
    moved = sum(a.size * a.dtype.itemsize for a in args + hbm)
    vmem, far = pl.BlockSpec(memory_space=pltpu.VMEM), pl.BlockSpec(memory_space=pl.ANY)
    result = pl.pallas_call(
        kernel,
        out_shape=shapes,
        in_specs=[vmem] * len(args) + [far] * len(hbm),
        out_specs=[far if k in hbm_outs else vmem for k in range(len(shapes))],
        scratch_shapes=list(scratch) + ([pltpu.SemaphoreType.DMA((copies,))] if copies else []),
        compiler_params=pltpu.CompilerParams(vmem_limit_bytes=20 * 1024 * 1024),
        cost_estimate=pl.CostEstimate(flops=flops, bytes_accessed=moved, transcendentals=0),
        name=name,
    )(*args, *hbm)
    return result if len(result) > 1 else result[0]


def steps(count):
    up = [(k, k + 1) for k in range(count - 1)]
    return up, [(b, a) for a, b in up]


def trades(count):
    even = [(k, k ^ 1) for k in range(count)]
    return even, [(k, ((k - 1) ^ 1) + 1) for k in range(1, count - 1)]


def per_device(
    fine_nodes, fine_edges, edge_src, edge_dst, send_rows, parents, coarse_src, coarse_dst,
    w_edge_in, w_edge_out, edge_gain, w_node_in, w_node_out, node_gain, w_cedge_in, w_cedge_out,
    w_cnode_in, w_cnode_out, coarse_gain, w_up_in, w_up_out, up_gain,
):
    count_x, count_y = lax.axis_size("gx"), lax.axis_size("gy")
    src, dst = edge_src.reshape(8, 128), edge_dst.reshape(8, 128)
    csrc, cdst = coarse_src.reshape(8, 128), coarse_dst.reshape(8, 128)
    owner = parents.reshape(4, 128)
    edge_gain, node_gain = edge_gain.reshape(1, 512), node_gain.reshape(1, 512)
    coarse_gain, up_gain = coarse_gain.reshape(1, 512), up_gain.reshape(1, 512)
    block = pltpu.VMEM((512, 512), BF16)

    far, before, after, near = call(
        outgoing_kernel, [((96, 512), BF16), ((32, 512), BF16), ((32, 512), BF16), ((96, 512), BF16)],
        hbm=(fine_nodes, send_rows[0]), scratch=[block, pltpu.VMEM((8, 32), I32)], copies=2,
        flops=100 * 2 * 256 * 512 * 512, name="outgoing",
    )
    even_x, odd_x = trades(count_x)
    even_y, odd_y = trades(count_y)
    far = lax.ppermute(far, "gx", odd_x)
    near = lax.ppermute(near, "gx", even_x)
    gathered = call(
        tables_kernel, [((1024, 512), F32)], fine_nodes, src, dst, w_edge_in, held=(0,),
        flops=2 * 6 * 512**3, name="tables",
    )
    far, near, gathered = lax.optimization_barrier((far, near, gathered))
    side_a = lax.ppermute(jnp.concatenate([far[64:96], after, near[64:96]], 0), "gy", even_y)
    side_b = lax.ppermute(jnp.concatenate([far[0:32], before, near[0:32]], 0), "gy", odd_y)
    square = ((512, 512), BF16)
    pre, node_pre, edges, w_source, w_summed = call(
        edges_kernel, [((1024, 512), F32), ((512, 512), F32), ((1024, 512), BF16), square, square],
        fine_nodes, hold(gathered), hbm=(fine_edges, w_edge_in, w_node_in), held=(0, 1, 2, 3, 4),
        scratch=[block, block], copies=6, flops=2 * 3 * 512**3, name="edges",
    )
    edges_out, level_one, pooled = call(
        after_halo_kernel, [((1024, 512), BF16), square, ((COARSE, 512), BF16)],
        far, near, side_a, side_b, hold(pre), hold(node_pre), fine_nodes, hold(edges), src, dst, owner,
        hold(w_source), w_edge_out, edge_gain, hold(w_summed), w_node_out, node_gain,
        hbm_outs=(0,), scratch=[pltpu.VMEM((1024, 512), BF16)], copies=1, flops=2 * 8 * 512**3, name="after_halo",
    )
    parts = lax.all_to_all(pooled, "gx", 0, 0, tiled=True)
    shares = call(
        share_kernel, [((count_x, COARSE // count_x, 512), BF16)], parts.reshape(count_x, -1, 512),
        flops=COARSE * 512, name="share",
    )
    zero = lax.all_to_all(shares, "gx", 0, 0, tiled=True).reshape(COARSE, 512)
    up_y, down_y = steps(count_y)
    left, right = lax.ppermute(zero, "gy", up_y), lax.ppermute(zero, "gy", down_y)
    pre, node_pre, up_pre, w_source, w_summed, w_lifted, w_last = call(
        own_kernel, [((1024, 512), F32), ((COARSE, 512), F32), ((512, 512), F32)] + [square] * 4,
        zero, csrc, cdst, level_one, w_cedge_in, hbm=(w_cedge_in, w_cnode_in, w_up_in, w_up_out),
        held=range(7), scratch=[block, block], copies=6, flops=2 * 5 * 512**3, name="own_column",
    )
    fine_out = call(
        coarse_kernel, [square],
        left, right, zero, hold(pre), hold(node_pre), hold(up_pre), csrc, cdst, owner, level_one,
        hold(w_source), w_cedge_out, hold(w_summed), w_cnode_out, coarse_gain, hold(w_lifted), hold(w_last), up_gain,
        hbm_outs=(0,), scratch=[block], copies=1, flops=2 * 9 * 512**3, name="coarse",
    )
    return fine_out, edges_out


def solution(mesh):
    fine, flat = P(("gx", "gy"), None), P(("gx", "gy"))
    return jax.shard_map(
        per_device,
        mesh=mesh,
        in_specs=(fine, fine, flat, flat, P(("gx", "gy"), None, None), flat, P("gy"), P("gy")) + (P(),) * 14,
        out_specs=(fine, fine),
        check_vma=False,
    )
```

```python
import jax
import jax.numpy as jnp
from jax import lax
from jax.experimental import pallas as pl
from jax.experimental.pallas import tpu as pltpu
from jax.sharding import PartitionSpec as P

COARSE = 256
BF16 = jnp.bfloat16
F32 = jnp.float32
I32 = jnp.int32


def dot(a, b):
    return jnp.dot(a, b, preferred_element_type=F32)


def silu(v):
    half = 0.5 * v
    return half + half * jnp.tanh(half)


def layer_norm(values):
    mean = jnp.mean(values, axis=-1, keepdims=True)
    centred = values - mean
    spread = jnp.mean(centred * centred, axis=-1, keepdims=True)
    return centred * lax.rsqrt(spread + 1e-05)


def mlp_tail(pre, w_out, gain):
    return layer_norm(dot(silu(pre).astype(BF16), w_out)) * gain


def pick(column, width, base=0):
    lanes = lax.broadcasted_iota(I32, (column.shape[0], width), 1) + base
    return jnp.where(lanes == column, 1.0, 0.0).astype(BF16)


def spread(row, height):
    rows = lax.broadcasted_iota(I32, (height, row.shape[1]), 0)
    return jnp.where(rows == row, 1.0, 0.0).astype(BF16)


def as_column(table):
    turned = jnp.transpose(table)
    return jnp.concatenate([turned[:, k : k + 1] for k in range(table.shape[0])], 0)


def as_row(table):
    return jnp.concatenate([table[k : k + 1, :] for k in range(table.shape[0])], 1)


def odd_place():
    return lax.axis_index("gx") % 2 == 1, lax.axis_index("gy") % 2 == 1


def fetch(sems, *pairs):
    copies = [pltpu.make_async_copy(a, b, sems.at[k]) for k, (a, b) in enumerate(pairs)]
    for copy in copies:
        copy.start()
    return copies


def outgoing_kernel(nodes_hbm, lists_hbm, far, before, after, near, nodes, lists, sems):
    got_lists, got_nodes = fetch(sems, (lists_hbm, lists), (nodes_hbm, nodes))
    got_lists.wait()
    odd_x, odd_y = odd_place()
    rows = lists[...]
    rows = jnp.where(odd_x, jnp.concatenate([rows[5:8], rows[3:5], rows[0:3]], 0), rows)
    rows = jnp.where(odd_y, jnp.concatenate([rows[k : k + 1] for k in (2, 1, 0, 4, 3, 7, 6, 5)], 0), rows)
    picks = jnp.transpose(rows)
    picks = jnp.concatenate([pick(picks[:, k : k + 1], 512) for k in range(8)], 0)
    got_nodes.wait()
    picked = dot(picks, nodes[...]).astype(BF16)
    far[...] = picked[0:96, :]
    before[...] = picked[96:128, :]
    after[...] = picked[128:160, :]
    near[...] = picked[160:256, :]


def tables_kernel(nodes, src, dst, w_in, gathered):
    nodes = nodes[...]
    src_proj = dot(nodes, w_in[512:1024, :]).astype(BF16)
    dst_proj = dot(nodes, w_in[1024:1536, :]).astype(BF16)
    part = dot(pick(as_column(src[...]), 512), src_proj)
    gathered[...] = part + dot(pick(as_column(dst[...]), 512), dst_proj)


def edges_kernel(
    nodes, gathered, edges_hbm, w_in_hbm, w_node_hbm, pre, node_pre, edges, w_source, w_summed, w_in, w_node, sems
):
    got = fetch(
        sems, (w_node_hbm.at[0:512], w_node), (w_in_hbm.at[0:512], w_in),
        (edges_hbm.at[0:512], edges.at[0:512]), (edges_hbm.at[512:1024], edges.at[512:1024]),
        (w_in_hbm.at[512:1024], w_source), (w_node_hbm.at[512:1024], w_summed),
    )
    got[0].wait()
    node_pre[...] = dot(nodes[...], w_node[...])
    got[1].wait()
    for c in range(2):
        rows = slice(512 * c, 512 * c + 512)
        got[2 + c].wait()
        pre[rows, :] = gathered[rows, :] + dot(edges[rows, :], w_in[...])
    got[4].wait()
    got[5].wait()


def after_halo_kernel(
    far, near, side_a, side_b, pre, node_pre, nodes, src, dst, parents,
    w_source, w_out, gain, w_summed, w_node_out, node_gain,
    message_out, level_one, pooled,
):
    received = jnp.concatenate(
        [
            side_a[64:96, :], near[32:64, :], side_b[64:96, :], side_a[32:64, :],
            side_b[32:64, :], side_a[0:32, :], far[32:64, :], side_b[0:32, :],
        ],
        0,
    )
    halo = dot(received, w_source[...]).astype(BF16)
    odd_x, odd_y = odd_place()
    slot = src[...] - 512
    k = slot >> 5
    turn_x = jnp.where(k < 3, k + 5, jnp.where(k > 4, k - 5, k))
    k = jnp.where(odd_x, turn_x, k)
    turn_y = jnp.where(
        (k == 0) | (k == 5), k + 2, jnp.where((k == 2) | (k == 7), k - 2, jnp.where(k == 3, 4, jnp.where(k == 4, 3, k)))
    )
    k = jnp.where(odd_y, turn_y, k)
    slot = jnp.where(slot < 0, -1, k * 32 + (slot & 31))
    part = pre[...] + dot(pick(as_column(slot), 256), halo)
    message = mlp_tail(part, w_out[...], gain[...])
    message_out[...] = message
    summed = dot(spread(as_row(dst[...]), 512), message.astype(BF16)).astype(BF16)
    part = node_pre[...] + dot(summed, w_summed[...])
    level = nodes[...].astype(F32) + mlp_tail(part, w_node_out[...], node_gain[...])
    level = level.astype(BF16)
    level_one[...] = level
    pooled[...] = dot(spread(as_row(parents[...]), COARSE), level).astype(BF16)


def share_kernel(parts, out):
    total = parts[0].astype(F32)
    for k in range(1, parts.shape[0]):
        total = total + parts[k].astype(F32)
    share = layer_norm(total).astype(BF16)
    for k in range(out.shape[0]):
        out[k] = share


def own_kernel(
    zero, csrc, cdst, level_one, edges, message, w_cin, w_nin_hbm, w_up_hbm,
    pre, node_pre, up_pre, w_summed, edges_hbm, w_nin, w_up, edges_out, sems,
):
    got = fetch(
        sems, (w_nin_hbm.at[0:512], w_nin), (w_up_hbm.at[0:512], w_up), (w_nin_hbm.at[512:1024], w_summed)
    )
    edges_out[...] = (edges[...].astype(F32) + message[...]).astype(BF16)
    sent = pltpu.make_async_copy(edges_out, edges_hbm, sems.at[3])
    sent.start()
    zero = zero[...]
    side_src = dot(zero, w_cin[0:512, :]).astype(BF16)
    side_dst = dot(zero, w_cin[512:1024, :]).astype(BF16)
    part = dot(pick(as_column(csrc[...]), COARSE, COARSE), side_src)
    pre[...] = part + dot(pick(as_column(cdst[...]), COARSE), side_dst)
    got[0].wait()
    node_pre[...] = dot(zero, w_nin[...])
    got[1].wait()
    up_pre[...] = dot(level_one[...], w_up[...])
    got[2].wait()
    sent.wait()


def first_is_right():
    odd_x, odd_y = odd_place()
    return odd_x == odd_y


def side_rows(side, right, csrc, w_source):
    side_src = dot(side[...], w_source[...]).astype(BF16)
    base = jnp.where(right, 2 * COARSE, 0)
    return dot(pick(as_column(csrc[...] - base), COARSE), side_src)


def first_kernel(side, pre, csrc, w_cin, w_up_hbm, w_up_out_hbm, both, w_lifted, w_up_out, sems):
    got = fetch(sems, (w_up_hbm.at[512:1024], w_lifted), (w_up_out_hbm, w_up_out))
    both[...] = pre[...] + side_rows(side, first_is_right(), csrc, w_cin.at[0:512])
    for copy in got:
        copy.wait()


def coarse_kernel(
    side, zero, pre, node_pre, up_pre, csrc, cdst, parents, level_one,
    w_cin, w_cout, w_summed, w_nout, coarse_gain, w_lifted, w_up_out, up_gain,
    out_hbm, out, sems,
):
    part = pre[...] + side_rows(side, jnp.logical_not(first_is_right()), csrc, w_cin.at[0:512])
    message = layer_norm(dot(silu(part).astype(BF16), w_cout[...]))
    summed = dot(spread(as_row(cdst[...]), COARSE), message.astype(BF16)).astype(BF16)
    part = node_pre[...] + dot(summed, w_summed[...])
    one = (zero[...].astype(F32) + mlp_tail(part, w_nout[...], coarse_gain[...])).astype(BF16)
    lifted = dot(pick(as_column(parents[...]), COARSE), one).astype(BF16)
    part = up_pre[...] + dot(lifted, w_lifted[...])
    tail = mlp_tail(part, w_up_out[...], up_gain[...])
    out[...] = (level_one[...].astype(F32) + tail).astype(BF16)
    (sent,) = fetch(sems, (out, out_hbm))
    sent.wait()


def kept(shape, dtype):
    return pltpu.VMEM(shape, dtype)


def hold(array):
    return pltpu.with_memory_space_constraint(array, pltpu.VMEM)


def call(kernel, outs, *args, hbm=(), hbm_outs=(), held=(), scratch=(), copies=0, flops=0, name=None):
    shapes = [kept(s, d) if k in held else jax.ShapeDtypeStruct(s, d) for k, (s, d) in enumerate(outs)]
    args = list(args)
    hbm = [pltpu.with_memory_space_constraint(a, pltpu.HBM) for a in hbm]
    moved = sum(a.size * a.dtype.itemsize for a in args + hbm)
    vmem, far = pl.BlockSpec(memory_space=pltpu.VMEM), pl.BlockSpec(memory_space=pl.ANY)
    result = pl.pallas_call(
        kernel,
        out_shape=shapes,
        in_specs=[vmem] * len(args) + [far] * len(hbm),
        out_specs=[far if k in hbm_outs else vmem for k in range(len(shapes))],
        scratch_shapes=list(scratch) + ([pltpu.SemaphoreType.DMA((copies,))] if copies else []),
        compiler_params=pltpu.CompilerParams(vmem_limit_bytes=20 * 1024 * 1024),
        cost_estimate=pl.CostEstimate(flops=flops, bytes_accessed=moved, transcendentals=0),
        name=name,
    )(*args, *hbm)
    return result if len(result) > 1 else result[0]


def trades(count):
    even = [(k, k ^ 1) for k in range(count)]
    return even, [(k, ((k - 1) ^ 1) + 1) for k in range(1, count - 1)]


def per_device(
    fine_nodes, fine_edges, edge_src, edge_dst, send_rows, parents, coarse_src, coarse_dst,
    w_edge_in, w_edge_out, edge_gain, w_node_in, w_node_out, node_gain, w_cedge_in, w_cedge_out,
    w_cnode_in, w_cnode_out, coarse_gain, w_up_in, w_up_out, up_gain,
):
    count_x, count_y = lax.axis_size("gx"), lax.axis_size("gy")
    src, dst = edge_src.reshape(8, 128), edge_dst.reshape(8, 128)
    csrc, cdst = coarse_src.reshape(8, 128), coarse_dst.reshape(8, 128)
    owner = parents.reshape(4, 128)
    edge_gain, node_gain = edge_gain.reshape(1, 512), node_gain.reshape(1, 512)
    coarse_gain, up_gain = coarse_gain.reshape(1, 512), up_gain.reshape(1, 512)
    block = pltpu.VMEM((512, 512), BF16)

    far, before, after, near = call(
        outgoing_kernel, [((96, 512), BF16), ((32, 512), BF16), ((32, 512), BF16), ((96, 512), BF16)],
        hbm=(fine_nodes, send_rows[0]), scratch=[block, pltpu.VMEM((8, 32), I32)], copies=2,
        flops=100 * 2 * 256 * 512 * 512, name="outgoing",
    )
    even_x, odd_x = trades(count_x)
    even_y, odd_y = trades(count_y)
    far = lax.ppermute(far, "gx", odd_x)
    near = lax.ppermute(near, "gx", even_x)
    gathered = call(
        tables_kernel, [((1024, 512), F32)], fine_nodes, src, dst, w_edge_in, held=(0,),
        flops=2 * 6 * 512**3, name="tables",
    )
    far, near, gathered = lax.optimization_barrier((far, near, gathered))
    side_a = lax.ppermute(jnp.concatenate([far[64:96], after, near[64:96]], 0), "gy", even_y)
    side_b = lax.ppermute(jnp.concatenate([far[0:32], before, near[0:32]], 0), "gy", odd_y)
    square = ((512, 512), BF16)
    pre, node_pre, edges, w_source, w_summed = call(
        edges_kernel, [((1024, 512), F32), ((512, 512), F32), ((1024, 512), BF16), square, square],
        fine_nodes, hold(gathered), hbm=(fine_edges, w_edge_in, w_node_in), held=(0, 1, 2, 3, 4),
        scratch=[block, block], copies=6, flops=2 * 3 * 512**3, name="edges",
    )
    message, level_one, pooled = call(
        after_halo_kernel, [((1024, 512), F32), square, ((COARSE, 512), BF16)],
        far, near, side_a, side_b, hold(pre), hold(node_pre), fine_nodes, src, dst, owner,
        hold(w_source), w_edge_out, edge_gain, hold(w_summed), w_node_out, node_gain,
        held=(0,), flops=2 * 8 * 512**3, name="after_halo",
    )
    parts = lax.all_to_all(pooled, "gx", 0, 0, tiled=True)
    shares = call(
        share_kernel, [((count_x, COARSE // count_x, 512), BF16)], parts.reshape(count_x, -1, 512),
        flops=COARSE * 512, name="share",
    )
    zero = lax.all_to_all(shares, "gx", 0, 0, tiled=True).reshape(COARSE, 512)
    sideways = [
        (i * count_y + j, i * count_y + to) for i in range(count_x) for j, to in (odd_y if i % 2 else even_y)
    ]
    first = lax.ppermute(zero, ("gx", "gy"), sideways)
    pre, node_pre, up_pre, w_summed, edges_out = call(
        own_kernel, [((1024, 512), F32), ((COARSE, 512), F32), ((512, 512), F32), square, ((1024, 512), BF16)],
        zero, csrc, cdst, level_one, hold(edges), hold(message), w_cedge_in, hbm=(w_cnode_in, w_up_in),
        held=range(4), hbm_outs=(4,), scratch=[block, block, pltpu.VMEM((1024, 512), BF16)], copies=4, flops=2 * 5 * 512**3, name="own_column",
    )
    first, pre = lax.optimization_barrier((first, pre))
    second = lax.ppermute(first, "gx", even_x)
    pre, w_lifted, w_last = call(
        first_kernel, [((1024, 512), F32), square, square], first, hold(pre), csrc, w_cedge_in,
        hbm=(w_up_in, w_up_out), held=range(3), copies=2, flops=2 * 2 * 512**3, name="first_side",
    )
    fine_out = call(
        coarse_kernel, [square],
        second, zero, hold(pre), hold(node_pre), hold(up_pre), csrc, cdst, owner, level_one,
        w_cedge_in, w_cedge_out, hold(w_summed), w_cnode_out, coarse_gain, hold(w_lifted), hold(w_last), up_gain,
        hbm_outs=(0,), scratch=[block], copies=1, flops=2 * 8 * 512**3, name="coarse",
    )
    return fine_out, edges_out


def solution(mesh):
    fine, flat = P(("gx", "gy"), None), P(("gx", "gy"))
    return jax.shard_map(
        per_device,
        mesh=mesh,
        in_specs=(fine, fine, flat, flat, P(("gx", "gy"), None, None), flat, P("gy"), P("gy")) + (P(),) * 14,
        out_specs=(fine, fine),
        check_vma=False,
    )
```

```python
import jax
import jax.numpy as jnp
from jax import lax
from jax.experimental import pallas as pl
from jax.experimental.pallas import tpu as pltpu
from jax.sharding import PartitionSpec as P

COARSE = 256
BF16 = jnp.bfloat16
F32 = jnp.float32
I32 = jnp.int32


def dot(a, b):
    return jnp.dot(a, b, preferred_element_type=F32)


def silu(v):
    half = 0.5 * v
    return half + half * jnp.tanh(half)


def layer_norm(values):
    mean = jnp.mean(values, axis=-1, keepdims=True)
    centred = values - mean
    spread = jnp.mean(centred * centred, axis=-1, keepdims=True)
    return centred * lax.rsqrt(spread + 1e-05)


def mlp_tail(pre, w_out, gain):
    return layer_norm(dot(silu(pre).astype(BF16), w_out)) * gain


def pick(column, width, base=0):
    lanes = lax.broadcasted_iota(I32, (column.shape[0], width), 1) + base
    return jnp.where(lanes == column, 1.0, 0.0).astype(BF16)


def spread(row, height):
    rows = lax.broadcasted_iota(I32, (height, row.shape[1]), 0)
    return jnp.where(rows == row, 1.0, 0.0).astype(BF16)


def as_column(table):
    turned = jnp.transpose(table)
    return jnp.concatenate([turned[:, k : k + 1] for k in range(table.shape[0])], 0)


def as_row(table):
    return jnp.concatenate([table[k : k + 1, :] for k in range(table.shape[0])], 1)


def odd_place():
    return lax.axis_index("gx") % 2 == 1, lax.axis_index("gy") % 2 == 1


def fetch(sems, *pairs):
    copies = [pltpu.make_async_copy(a, b, sems.at[k]) for k, (a, b) in enumerate(pairs)]
    for copy in copies:
        copy.start()
    return copies


def outgoing_kernel(nodes_hbm, lists_hbm, far, before, after, near, nodes, lists, sems):
    got_lists, got_nodes = fetch(sems, (lists_hbm, lists), (nodes_hbm, nodes))
    got_lists.wait()
    odd_x, odd_y = odd_place()
    rows = lists[...]
    rows = jnp.where(odd_x, jnp.concatenate([rows[5:8], rows[3:5], rows[0:3]], 0), rows)
    rows = jnp.where(odd_y, jnp.concatenate([rows[k : k + 1] for k in (2, 1, 0, 4, 3, 7, 6, 5)], 0), rows)
    picks = jnp.transpose(rows)
    picks = jnp.concatenate([pick(picks[:, k : k + 1], 512) for k in range(8)], 0)
    got_nodes.wait()
    picked = dot(picks, nodes[...]).astype(BF16)
    far[...] = picked[0:96, :]
    before[...] = picked[96:128, :]
    after[...] = picked[128:160, :]
    near[...] = picked[160:256, :]


def tables_kernel(nodes, src, dst, w_in, gathered, dst_spread):
    nodes = nodes[...]
    src_proj = dot(nodes, w_in[512:1024, :]).astype(BF16)
    dst_proj = dot(nodes, w_in[1024:1536, :]).astype(BF16)
    part = dot(pick(as_column(src[...]), 512), src_proj)
    gathered[...] = part + dot(pick(as_column(dst[...]), 512), dst_proj)
    dst_spread[...] = spread(as_row(dst[...]), 512)


def halo_slots(src):
    odd_x, odd_y = odd_place()
    slot = src - 512
    k = slot >> 5
    turn_x = jnp.where(k < 3, k + 5, jnp.where(k > 4, k - 5, k))
    k = jnp.where(odd_x, turn_x, k)
    turn_y = jnp.where(
        (k == 0) | (k == 5), k + 2, jnp.where((k == 2) | (k == 7), k - 2, jnp.where(k == 3, 4, jnp.where(k == 4, 3, k)))
    )
    k = jnp.where(odd_y, turn_y, k)
    slot = jnp.where(slot < 0, -1, k * 32 + (slot & 31))
    return slot


def edges_kernel(
    nodes, gathered, src, parents, edges_hbm, w_in_hbm, w_node_hbm,
    pre, node_pre, edges, w_source, w_summed, halo_pick, owner_spread, w_in, w_node, sems,
):
    got = fetch(
        sems, (w_node_hbm.at[0:512], w_node), (w_in_hbm.at[0:512], w_in),
        (edges_hbm.at[0:512], edges.at[0:512]), (edges_hbm.at[512:1024], edges.at[512:1024]),
        (w_in_hbm.at[512:1024], w_source), (w_node_hbm.at[512:1024], w_summed),
    )
    halo_pick[...] = pick(as_column(halo_slots(src[...])), 256)
    owner_spread[...] = spread(as_row(parents[...]), COARSE)
    got[0].wait()
    node_pre[...] = dot(nodes[...], w_node[...])
    got[1].wait()
    for c in range(2):
        rows = slice(512 * c, 512 * c + 512)
        got[2 + c].wait()
        pre[rows, :] = gathered[rows, :] + dot(edges[rows, :], w_in[...])
    got[4].wait()
    got[5].wait()


def after_halo_kernel(
    far, near, side_a, side_b, pre, node_pre, nodes, halo_pick, dst_spread, owner_spread,
    w_source, w_out, gain, w_summed, w_node_out, node_gain,
    message_out, level_one, pooled,
):
    received = jnp.concatenate(
        [
            side_a[64:96, :], near[32:64, :], side_b[64:96, :], side_a[32:64, :],
            side_b[32:64, :], side_a[0:32, :], far[32:64, :], side_b[0:32, :],
        ],
        0,
    )
    halo = dot(received, w_source[...]).astype(BF16)
    part = pre[...] + dot(halo_pick[...], halo)
    message = mlp_tail(part, w_out[...], gain[...])
    message_out[...] = message
    summed = dot(dst_spread[...], message.astype(BF16)).astype(BF16)
    part = node_pre[...] + dot(summed, w_summed[...])
    level = nodes[...].astype(F32) + mlp_tail(part, w_node_out[...], node_gain[...])
    level = level.astype(BF16)
    level_one[...] = level
    pooled[...] = dot(owner_spread[...], level).astype(BF16)


def share_kernel(parts, out):
    total = parts[0].astype(F32)
    for k in range(1, parts.shape[0]):
        total = total + parts[k].astype(F32)
    share = layer_norm(total).astype(BF16)
    for k in range(out.shape[0]):
        out[k] = share


def own_kernel(
    zero, csrc, cdst, parents, level_one, edges, message, w_cin, w_nin_hbm, w_up_hbm,
    pre, node_pre, up_pre, edges_hbm, first_pick, second_pick, dst_spread, owner_pick,
    w_nin, w_up, edges_out, sems,
):
    got = fetch(sems, (w_nin_hbm.at[0:512], w_nin), (w_up_hbm.at[0:512], w_up))
    edges_out[...] = (edges[...].astype(F32) + message[...]).astype(BF16)
    sent = pltpu.make_async_copy(edges_out, edges_hbm, sems.at[2])
    sent.start()
    zero = zero[...]
    side_src = dot(zero, w_cin[0:512, :]).astype(BF16)
    side_dst = dot(zero, w_cin[512:1024, :]).astype(BF16)
    part = dot(pick(as_column(csrc[...]), COARSE, COARSE), side_src)
    pre[...] = part + dot(pick(as_column(cdst[...]), COARSE), side_dst)
    right = first_is_right()
    first_pick[...] = side_pick(right, csrc[...])
    second_pick[...] = side_pick(jnp.logical_not(right), csrc[...])
    dst_spread[...] = spread(as_row(cdst[...]), COARSE)
    owner_pick[...] = pick(as_column(parents[...]), COARSE)
    got[0].wait()
    node_pre[...] = dot(zero, w_nin[...])
    got[1].wait()
    up_pre[...] = dot(level_one[...], w_up[...])
    sent.wait()


def first_is_right():
    odd_x, odd_y = odd_place()
    return odd_x == odd_y


def side_pick(right, csrc):
    return pick(as_column(csrc - jnp.where(right, 2 * COARSE, 0)), COARSE)


def first_kernel(side, pre, first_pick, w_cin, w_nin_hbm, both, w_summed, sems):
    (got,) = fetch(sems, (w_nin_hbm.at[512:1024], w_summed))
    side_src = dot(side[...], w_cin[0:512, :]).astype(BF16)
    both[...] = pre[...] + dot(first_pick[...], side_src)
    got.wait()


def coarse_kernel(
    side, zero, pre, node_pre, up_pre, second_pick, dst_spread, owner_pick, level_one,
    w_cin, w_cout, w_summed, w_nout, coarse_gain, up_gain, w_up_hbm, w_up_out_hbm,
    out_hbm, out, w_lifted, w_up_out, sems,
):
    got = fetch(sems, (w_up_hbm.at[512:1024], w_lifted), (w_up_out_hbm, w_up_out))
    side_src = dot(side[...], w_cin[0:512, :]).astype(BF16)
    part = pre[...] + dot(second_pick[...], side_src)
    message = layer_norm(dot(silu(part).astype(BF16), w_cout[...]))
    summed = dot(dst_spread[...], message.astype(BF16)).astype(BF16)
    part = node_pre[...] + dot(summed, w_summed[...])
    one = (zero[...].astype(F32) + mlp_tail(part, w_nout[...], coarse_gain[...])).astype(BF16)
    lifted = dot(owner_pick[...], one).astype(BF16)
    got[0].wait()
    part = up_pre[...] + dot(lifted, w_lifted[...])
    got[1].wait()
    tail = mlp_tail(part, w_up_out[...], up_gain[...])
    out[...] = (level_one[...].astype(F32) + tail).astype(BF16)
    (sent,) = fetch(sems, (out, out_hbm))
    sent.wait()


def kept(shape, dtype):
    return pltpu.VMEM(shape, dtype)


def hold(array):
    return pltpu.with_memory_space_constraint(array, pltpu.VMEM)


def call(kernel, outs, *args, hbm=(), hbm_outs=(), held=(), scratch=(), copies=0, flops=0, name=None):
    shapes = [kept(s, d) if k in held else jax.ShapeDtypeStruct(s, d) for k, (s, d) in enumerate(outs)]
    args = list(args)
    hbm = [pltpu.with_memory_space_constraint(a, pltpu.HBM) for a in hbm]
    moved = sum(a.size * a.dtype.itemsize for a in args + hbm)
    vmem, far = pl.BlockSpec(memory_space=pltpu.VMEM), pl.BlockSpec(memory_space=pl.ANY)
    result = pl.pallas_call(
        kernel,
        out_shape=shapes,
        in_specs=[vmem] * len(args) + [far] * len(hbm),
        out_specs=[far if k in hbm_outs else vmem for k in range(len(shapes))],
        scratch_shapes=list(scratch) + ([pltpu.SemaphoreType.DMA((copies,))] if copies else []),
        compiler_params=pltpu.CompilerParams(vmem_limit_bytes=20 * 1024 * 1024),
        cost_estimate=pl.CostEstimate(flops=flops, bytes_accessed=moved, transcendentals=0),
        name=name,
    )(*args, *hbm)
    return result if len(result) > 1 else result[0]


def trades(count):
    even = [(k, k ^ 1) for k in range(count)]
    return even, [(k, ((k - 1) ^ 1) + 1) for k in range(1, count - 1)]


def per_device(
    fine_nodes, fine_edges, edge_src, edge_dst, send_rows, parents, coarse_src, coarse_dst,
    w_edge_in, w_edge_out, edge_gain, w_node_in, w_node_out, node_gain, w_cedge_in, w_cedge_out,
    w_cnode_in, w_cnode_out, coarse_gain, w_up_in, w_up_out, up_gain,
):
    count_x, count_y = lax.axis_size("gx"), lax.axis_size("gy")
    src, dst = edge_src.reshape(8, 128), edge_dst.reshape(8, 128)
    csrc, cdst = coarse_src.reshape(8, 128), coarse_dst.reshape(8, 128)
    owner = parents.reshape(4, 128)
    edge_gain, node_gain = edge_gain.reshape(1, 512), node_gain.reshape(1, 512)
    coarse_gain, up_gain = coarse_gain.reshape(1, 512), up_gain.reshape(1, 512)
    block = pltpu.VMEM((512, 512), BF16)

    far, before, after, near = call(
        outgoing_kernel, [((96, 512), BF16), ((32, 512), BF16), ((32, 512), BF16), ((96, 512), BF16)],
        hbm=(fine_nodes, send_rows[0]), scratch=[block, pltpu.VMEM((8, 32), I32)], copies=2,
        flops=100 * 2 * 256 * 512 * 512, name="outgoing",
    )
    even_x, odd_x = trades(count_x)
    even_y, odd_y = trades(count_y)
    far = lax.ppermute(far, "gx", odd_x)
    near = lax.ppermute(near, "gx", even_x)
    gathered, dst_spread = call(
        tables_kernel, [((1024, 512), F32), ((512, 1024), BF16)], fine_nodes, src, dst, w_edge_in, held=(0, 1),
        flops=2 * 6 * 512**3, name="tables",
    )
    far, near, gathered = lax.optimization_barrier((far, near, gathered))
    side_a = lax.ppermute(jnp.concatenate([far[64:96], after, near[64:96]], 0), "gy", even_y)
    side_b = lax.ppermute(jnp.concatenate([far[0:32], before, near[0:32]], 0), "gy", odd_y)
    square = ((512, 512), BF16)
    pre, node_pre, edges, w_source, w_summed, halo_pick, owner_spread = call(
        edges_kernel,
        [((1024, 512), F32), ((512, 512), F32), ((1024, 512), BF16), square, square]
        + [((1024, 256), BF16), ((COARSE, 512), BF16)],
        fine_nodes, hold(gathered), src, owner, hbm=(fine_edges, w_edge_in, w_node_in), held=range(7),
        scratch=[block, block], copies=6, flops=2 * 3 * 512**3, name="edges",
    )
    message, level_one, pooled = call(
        after_halo_kernel, [((1024, 512), F32), square, ((COARSE, 512), BF16)],
        far, near, side_a, side_b, hold(pre), hold(node_pre), fine_nodes,
        hold(halo_pick), hold(dst_spread), hold(owner_spread),
        hold(w_source), w_edge_out, edge_gain, hold(w_summed), w_node_out, node_gain,
        held=(0,), flops=2 * 8 * 512**3, name="after_halo",
    )
    parts = lax.all_to_all(pooled, "gx", 0, 0, tiled=True)
    shares = call(
        share_kernel, [((count_x, COARSE // count_x, 512), BF16)], parts.reshape(count_x, -1, 512),
        flops=COARSE * 512, name="share",
    )
    zero = lax.all_to_all(shares, "gx", 0, 0, tiled=True).reshape(COARSE, 512)
    sideways = [
        (i * count_y + j, i * count_y + to) for i in range(count_x) for j, to in (odd_y if i % 2 else even_y)
    ]
    first = lax.ppermute(zero, ("gx", "gy"), sideways)
    picks = [((1024, COARSE), BF16)] * 2 + [((COARSE, 1024), BF16), ((512, COARSE), BF16)]
    pre, node_pre, up_pre, edges_out, first_pick, second_pick, dst_spread, owner_pick = call(
        own_kernel,
        [((1024, 512), F32), ((COARSE, 512), F32), ((512, 512), F32), ((1024, 512), BF16)] + picks,
        zero, csrc, cdst, owner, level_one, hold(edges), hold(message), w_cedge_in, hbm=(w_cnode_in, w_up_in),
        held=(0, 1, 2, 4, 5, 6, 7), hbm_outs=(3,), scratch=[block, block, pltpu.VMEM((1024, 512), BF16)], copies=3, flops=2 * 5 * 512**3, name="own_column",
    )
    first, pre = lax.optimization_barrier((first, pre))
    second = lax.ppermute(first, "gx", even_x)
    pre, w_summed = call(
        first_kernel, [((1024, 512), F32), square], first, hold(pre), hold(first_pick), w_cedge_in,
        hbm=(w_cnode_in,), held=(0, 1), copies=1, flops=2 * 2 * 512**3, name="first_side",
    )
    fine_out = call(
        coarse_kernel, [square],
        second, zero, hold(pre), hold(node_pre), hold(up_pre), hold(second_pick), hold(dst_spread), hold(owner_pick),
        level_one, w_cedge_in, w_cedge_out, hold(w_summed), w_cnode_out, coarse_gain, up_gain,
        hbm=(w_up_in, w_up_out), hbm_outs=(0,), scratch=[block] * 3, copies=2,
        flops=2 * 8 * 512**3, name="coarse",
    )
    return fine_out, edges_out


def solution(mesh):
    fine, flat = P(("gx", "gy"), None), P(("gx", "gy"))
    return jax.shard_map(
        per_device,
        mesh=mesh,
        in_specs=(fine, fine, flat, flat, P(("gx", "gy"), None, None), flat, P("gy"), P("gy")) + (P(),) * 14,
        out_specs=(fine, fine),
        check_vma=False,
    )
```

```python
import jax
import jax.numpy as jnp
from jax import lax
from jax.experimental import pallas as pl
from jax.experimental.pallas import tpu as pltpu
from jax.sharding import PartitionSpec as P

COARSE = 256
BF16 = jnp.bfloat16
F32 = jnp.float32
I32 = jnp.int32


def dot(a, b):
    return jnp.dot(a, b, preferred_element_type=F32)


def silu(v):
    half = 0.5 * v
    return half + half * jnp.tanh(half)


def layer_norm(values):
    mean = jnp.mean(values, axis=-1, keepdims=True)
    centred = values - mean
    spread = jnp.mean(centred * centred, axis=-1, keepdims=True)
    return centred * lax.rsqrt(spread + 1e-05)


def mlp_tail(pre, w_out, gain):
    return layer_norm(dot(silu(pre).astype(BF16), w_out)) * gain


def pick(column, width, base=0):
    lanes = lax.broadcasted_iota(I32, (column.shape[0], width), 1) + base
    return jnp.where(lanes == column, 1.0, 0.0).astype(BF16)


def spread(row, height):
    rows = lax.broadcasted_iota(I32, (height, row.shape[1]), 0)
    return jnp.where(rows == row, 1.0, 0.0).astype(BF16)


def as_column(table):
    turned = jnp.transpose(table)
    return jnp.concatenate([turned[:, k : k + 1] for k in range(table.shape[0])], 0)


def as_row(table):
    return jnp.concatenate([table[k : k + 1, :] for k in range(table.shape[0])], 1)


def odd_place():
    return lax.axis_index("gx") % 2 == 1, lax.axis_index("gy") % 2 == 1


def fetch(sems, *pairs):
    copies = [pltpu.make_async_copy(a, b, sems.at[k]) for k, (a, b) in enumerate(pairs)]
    for copy in copies:
        copy.start()
    return copies


def outgoing_kernel(nodes_hbm, lists_hbm, far, before, after, near, nodes, lists, sems):
    got_lists, got_nodes = fetch(sems, (lists_hbm, lists), (nodes_hbm, nodes))
    got_lists.wait()
    odd_x, odd_y = odd_place()
    rows = lists[...]
    rows = jnp.where(odd_x, jnp.concatenate([rows[5:8], rows[3:5], rows[0:3]], 0), rows)
    rows = jnp.where(odd_y, jnp.concatenate([rows[k : k + 1] for k in (2, 1, 0, 4, 3, 7, 6, 5)], 0), rows)
    picks = jnp.transpose(rows)
    picks = jnp.concatenate([pick(picks[:, k : k + 1], 512) for k in range(8)], 0)
    got_nodes.wait()
    picked = dot(picks, nodes[...]).astype(BF16)
    far[...] = picked[0:96, :]
    before[...] = picked[96:128, :]
    after[...] = picked[128:160, :]
    near[...] = picked[160:256, :]


def tables_kernel(nodes, src, dst, w_in, gathered):
    nodes = nodes[...]
    src_proj = dot(nodes, w_in[512:1024, :]).astype(BF16)
    dst_proj = dot(nodes, w_in[1024:1536, :]).astype(BF16)
    part = dot(pick(as_column(src[...]), 512), src_proj)
    gathered[...] = part + dot(pick(as_column(dst[...]), 512), dst_proj)


def halo_slots(src):
    odd_x, odd_y = odd_place()
    slot = src - 512
    k = slot >> 5
    turn_x = jnp.where(k < 3, k + 5, jnp.where(k > 4, k - 5, k))
    k = jnp.where(odd_x, turn_x, k)
    turn_y = jnp.where(
        (k == 0) | (k == 5), k + 2, jnp.where((k == 2) | (k == 7), k - 2, jnp.where(k == 3, 4, jnp.where(k == 4, 3, k)))
    )
    k = jnp.where(odd_y, turn_y, k)
    slot = jnp.where(slot < 0, -1, k * 32 + (slot & 31))
    return slot


def edges_kernel(
    nodes, gathered, src, dst, parents, edges_hbm, w_in_hbm, w_node_hbm,
    pre, node_pre, edges, w_source, w_summed, halo_pick, owner_spread, dst_spread, w_in, w_node, sems,
):
    got = fetch(
        sems, (w_node_hbm.at[0:512], w_node), (w_in_hbm.at[0:512], w_in),
        (edges_hbm.at[0:512], edges.at[0:512]), (edges_hbm.at[512:1024], edges.at[512:1024]),
        (w_in_hbm.at[512:1024], w_source), (w_node_hbm.at[512:1024], w_summed),
    )
    dst_spread[...] = spread(as_row(dst[...]), 512)
    halo_pick[...] = pick(as_column(halo_slots(src[...])), 256)
    owner_spread[...] = spread(as_row(parents[...]), COARSE)
    got[0].wait()
    node_pre[...] = dot(nodes[...], w_node[...])
    got[1].wait()
    for c in range(2):
        rows = slice(512 * c, 512 * c + 512)
        got[2 + c].wait()
        pre[rows, :] = gathered[rows, :] + dot(edges[rows, :], w_in[...])
    got[4].wait()
    got[5].wait()


def after_halo_kernel(
    far, near, side_a, side_b, pre, node_pre, nodes, halo_pick, dst_spread, owner_spread,
    w_source, w_out, gain, w_summed, w_node_out, node_gain,
    message_out, level_one, pooled,
):
    received = jnp.concatenate(
        [
            side_a[64:96, :], near[32:64, :], side_b[64:96, :], side_a[32:64, :],
            side_b[32:64, :], side_a[0:32, :], far[32:64, :], side_b[0:32, :],
        ],
        0,
    )
    halo = dot(received, w_source[...]).astype(BF16)
    part = pre[...] + dot(halo_pick[...], halo)
    message = mlp_tail(part, w_out[...], gain[...])
    message_out[...] = message
    summed = dot(dst_spread[...], message.astype(BF16)).astype(BF16)
    part = node_pre[...] + dot(summed, w_summed[...])
    level = nodes[...].astype(F32) + mlp_tail(part, w_node_out[...], node_gain[...])
    level = level.astype(BF16)
    level_one[...] = level
    pooled[...] = dot(owner_spread[...], level).astype(BF16)


def share_kernel(parts, out):
    total = parts[0].astype(F32)
    for k in range(1, parts.shape[0]):
        total = total + parts[k].astype(F32)
    share = layer_norm(total).astype(BF16)
    for k in range(out.shape[0]):
        out[k] = share


def own_kernel(
    zero, csrc, cdst, parents, level_one, edges, message, w_cin, w_nin_hbm, w_up_hbm, w_up_out_hbm,
    pre, node_pre, up_pre, edges_hbm, first_pick, second_pick, dst_spread, owner_pick, w_summed, w_lifted, w_up_out,
    w_nin, w_up, edges_out, sems,
):
    got = fetch(
        sems, (w_nin_hbm.at[0:512], w_nin), (w_up_hbm.at[0:512], w_up), (w_nin_hbm.at[512:1024], w_summed),
        (w_up_hbm.at[512:1024], w_lifted), (w_up_out_hbm, w_up_out),
    )
    edges_out[...] = (edges[...].astype(F32) + message[...]).astype(BF16)
    sent = pltpu.make_async_copy(edges_out, edges_hbm, sems.at[5])
    sent.start()
    zero = zero[...]
    side_src = dot(zero, w_cin[0:512, :]).astype(BF16)
    side_dst = dot(zero, w_cin[512:1024, :]).astype(BF16)
    part = dot(pick(as_column(csrc[...]), COARSE, COARSE), side_src)
    pre[...] = part + dot(pick(as_column(cdst[...]), COARSE), side_dst)
    right = first_is_right()
    first_pick[...] = side_pick(right, csrc[...])
    second_pick[...] = side_pick(jnp.logical_not(right), csrc[...])
    dst_spread[...] = spread(as_row(cdst[...]), COARSE)
    owner_pick[...] = pick(as_column(parents[...]), COARSE)
    got[0].wait()
    node_pre[...] = dot(zero, w_nin[...])
    got[1].wait()
    up_pre[...] = dot(level_one[...], w_up[...])
    for copy in got[2:]:
        copy.wait()
    sent.wait()


def first_is_right():
    odd_x, odd_y = odd_place()
    return odd_x == odd_y


def side_pick(right, csrc):
    return pick(as_column(csrc - jnp.where(right, 2 * COARSE, 0)), COARSE)


def first_kernel(side, pre, first_pick, w_cin, both):
    side_src = dot(side[...], w_cin[0:512, :]).astype(BF16)
    both[...] = pre[...] + dot(first_pick[...], side_src)


def coarse_kernel(
    side, zero, pre, node_pre, up_pre, second_pick, dst_spread, owner_pick, level_one,
    w_cin, w_cout, w_summed, w_nout, coarse_gain, w_lifted, w_up_out, up_gain,
    out_hbm, out, sems,
):
    side_src = dot(side[...], w_cin[0:512, :]).astype(BF16)
    part = pre[...] + dot(second_pick[...], side_src)
    message = layer_norm(dot(silu(part).astype(BF16), w_cout[...]))
    summed = dot(dst_spread[...], message.astype(BF16)).astype(BF16)
    part = node_pre[...] + dot(summed, w_summed[...])
    one = (zero[...].astype(F32) + mlp_tail(part, w_nout[...], coarse_gain[...])).astype(BF16)
    lifted = dot(owner_pick[...], one).astype(BF16)
    part = up_pre[...] + dot(lifted, w_lifted[...])
    tail = mlp_tail(part, w_up_out[...], up_gain[...])
    out[...] = (level_one[...].astype(F32) + tail).astype(BF16)
    (sent,) = fetch(sems, (out, out_hbm))
    sent.wait()


def kept(shape, dtype):
    return pltpu.VMEM(shape, dtype)


def hold(array):
    return pltpu.with_memory_space_constraint(array, pltpu.VMEM)


def call(kernel, outs, *args, hbm=(), hbm_outs=(), held=(), scratch=(), copies=0, flops=0, name=None):
    shapes = [kept(s, d) if k in held else jax.ShapeDtypeStruct(s, d) for k, (s, d) in enumerate(outs)]
    args = list(args)
    hbm = [pltpu.with_memory_space_constraint(a, pltpu.HBM) for a in hbm]
    moved = sum(a.size * a.dtype.itemsize for a in args + hbm)
    vmem, far = pl.BlockSpec(memory_space=pltpu.VMEM), pl.BlockSpec(memory_space=pl.ANY)
    result = pl.pallas_call(
        kernel,
        out_shape=shapes,
        in_specs=[vmem] * len(args) + [far] * len(hbm),
        out_specs=[far if k in hbm_outs else vmem for k in range(len(shapes))],
        scratch_shapes=list(scratch) + ([pltpu.SemaphoreType.DMA((copies,))] if copies else []),
        compiler_params=pltpu.CompilerParams(vmem_limit_bytes=20 * 1024 * 1024),
        cost_estimate=pl.CostEstimate(flops=flops, bytes_accessed=moved, transcendentals=0),
        name=name,
    )(*args, *hbm)
    return result if len(result) > 1 else result[0]


def trades(count):
    even = [(k, k ^ 1) for k in range(count)]
    return even, [(k, ((k - 1) ^ 1) + 1) for k in range(1, count - 1)]


def per_device(
    fine_nodes, fine_edges, edge_src, edge_dst, send_rows, parents, coarse_src, coarse_dst,
    w_edge_in, w_edge_out, edge_gain, w_node_in, w_node_out, node_gain, w_cedge_in, w_cedge_out,
    w_cnode_in, w_cnode_out, coarse_gain, w_up_in, w_up_out, up_gain,
):
    count_x, count_y = lax.axis_size("gx"), lax.axis_size("gy")
    src, dst = edge_src.reshape(8, 128), edge_dst.reshape(8, 128)
    csrc, cdst = coarse_src.reshape(8, 128), coarse_dst.reshape(8, 128)
    owner = parents.reshape(4, 128)
    edge_gain, node_gain = edge_gain.reshape(1, 512), node_gain.reshape(1, 512)
    coarse_gain, up_gain = coarse_gain.reshape(1, 512), up_gain.reshape(1, 512)
    block = pltpu.VMEM((512, 512), BF16)

    far, before, after, near = call(
        outgoing_kernel, [((96, 512), BF16), ((32, 512), BF16), ((32, 512), BF16), ((96, 512), BF16)],
        hbm=(fine_nodes, send_rows[0]), scratch=[block, pltpu.VMEM((8, 32), I32)], copies=2,
        flops=100 * 2 * 256 * 512 * 512, name="outgoing",
    )
    even_x, odd_x = trades(count_x)
    even_y, odd_y = trades(count_y)
    far = lax.ppermute(far, "gx", odd_x)
    near = lax.ppermute(near, "gx", even_x)
    gathered = call(
        tables_kernel, [((1024, 512), F32)], fine_nodes, src, dst, w_edge_in, held=(0,),
        flops=2 * 6 * 512**3, name="tables",
    )
    far, near, gathered = lax.optimization_barrier((far, near, gathered))
    side_a = lax.ppermute(jnp.concatenate([far[64:96], after, near[64:96]], 0), "gy", even_y)
    side_b = lax.ppermute(jnp.concatenate([far[0:32], before, near[0:32]], 0), "gy", odd_y)
    square = ((512, 512), BF16)
    pre, node_pre, edges, w_source, w_summed, halo_pick, owner_spread, edge_spread = call(
        edges_kernel,
        [((1024, 512), F32), ((512, 512), F32), ((1024, 512), BF16), square, square]
        + [((1024, 256), BF16), ((COARSE, 512), BF16), ((512, 1024), BF16)],
        fine_nodes, hold(gathered), src, dst, owner, hbm=(fine_edges, w_edge_in, w_node_in), held=range(8),
        scratch=[block, block], copies=6, flops=2 * 3 * 512**3, name="edges",
    )
    message, level_one, pooled = call(
        after_halo_kernel, [((1024, 512), F32), square, ((COARSE, 512), BF16)],
        far, near, side_a, side_b, hold(pre), hold(node_pre), fine_nodes,
        hold(halo_pick), hold(edge_spread), hold(owner_spread),
        hold(w_source), w_edge_out, edge_gain, hold(w_summed), w_node_out, node_gain,
        held=(0,), flops=2 * 8 * 512**3, name="after_halo",
    )
    parts = lax.all_to_all(pooled, "gx", 0, 0, tiled=True)
    shares = call(
        share_kernel, [((count_x, COARSE // count_x, 512), BF16)], parts.reshape(count_x, -1, 512),
        flops=COARSE * 512, name="share",
    )
    zero = lax.all_to_all(shares, "gx", 0, 0, tiled=True).reshape(COARSE, 512)
    sideways = [
        (i * count_y + j, i * count_y + to) for i in range(count_x) for j, to in (odd_y if i % 2 else even_y)
    ]
    first = lax.ppermute(zero, ("gx", "gy"), sideways)
    picks = [((1024, COARSE), BF16)] * 2 + [((COARSE, 1024), BF16), ((512, COARSE), BF16)]
    pre, node_pre, up_pre, edges_out, first_pick, second_pick, dst_spread, owner_pick, *late = call(
        own_kernel,
        [((1024, 512), F32), ((COARSE, 512), F32), ((512, 512), F32), ((1024, 512), BF16)] + picks + [square] * 3,
        zero, csrc, cdst, owner, level_one, hold(edges), hold(message), w_cedge_in, hbm=(w_cnode_in, w_up_in, w_up_out),
        held=(0, 1, 2, *range(4, 11)), hbm_outs=(3,), scratch=[block, block, pltpu.VMEM((1024, 512), BF16)], copies=6, flops=2 * 5 * 512**3, name="own_column",
    )
    first, pre = lax.optimization_barrier((first, pre))
    second = lax.ppermute(first, "gx", even_x)
    pre = call(
        first_kernel, [((1024, 512), F32)], first, hold(pre), hold(first_pick), w_cedge_in, held=(0,),
        flops=2 * 2 * 512**3, name="first_side",
    )
    w_summed, w_lifted, w_last = (hold(weight) for weight in late)
    fine_out = call(
        coarse_kernel, [square],
        second, zero, hold(pre), hold(node_pre), hold(up_pre), hold(second_pick), hold(dst_spread), hold(owner_pick),
        level_one, w_cedge_in, w_cedge_out, w_summed, w_cnode_out, coarse_gain, w_lifted, w_last, up_gain,
        hbm_outs=(0,), scratch=[block], copies=1, flops=2 * 8 * 512**3, name="coarse",
    )
    return fine_out, edges_out


def solution(mesh):
    fine, flat = P(("gx", "gy"), None), P(("gx", "gy"))
    return jax.shard_map(
        per_device,
        mesh=mesh,
        in_specs=(fine, fine, flat, flat, P(("gx", "gy"), None, None), flat, P("gy"), P("gy")) + (P(),) * 14,
        out_specs=(fine, fine),
        check_vma=False,
    )
```
